32 devices in a mesh: outer: 8 (over z, x), inner: 4 (over y, core).
Axes of the slice: x: 2, y: 2, z: 4, core: 2. Of those that a mesh axis runs over, the one named last changes fastest.
Arguments:
- queries: bfloat16 [8192, 1024], P(('outer', 'inner')), may hold values from -48 to 48
- keys: bfloat16 [8192, 128], P(('outer', 'inner')), may hold values from -4 to 4
- values: bfloat16 [8192, 128], P(('outer', 'inner')), may hold values from -6 to 6
- reflect: bfloat16 [8192, 128], P(('outer', 'inner')), may hold values from -6 to 6
- reflect_logit: float32 [8192], P(('outer', 'inner')), may hold values from -8 to 8
- doc_of_block: int32 [32], replicated, may hold values from 0 to 15, never falling along the last dimension, each value on 1 to 4 neighbouring positions
Outputs:
- attended: bfloat16 [8192, 1024], P(('outer', 'inner'))
The draws below stay inside these ranges and needn't reach their ends.
Inputs may be any that keep to these rules, and one draw needn't show every extreme that they name: `doc_of_block`: document numbers never fall along the blocks; every document covers 1 to 4 consecutive blocks, and one covers exactly 4.
All inputs are finite; a program needn't handle non-finite values.
Results may differ from the reference program's by a relative error of at most 0.017.
Values may be sent and summed in bfloat16 or wider, within the bound.
No kernel may reach another device: no remote copies, remote signals or barrier semaphores. Data moves between devices by JAX's collectives and lax.ppermute only.
A program may use at most 64 MiB of HBM per device.

```python
import math
import jax
import jax.numpy as jnp
import numpy as np
from jax import lax

HEAD = 128
QHEADS = 8
TOK_DEV = 256
BLOCKS = 32
TOKENS = 8192
MOST = 4


def joint_draw(key):
    query_seed = jax.random.fold_in(key, 101)
    key_seed = jax.random.fold_in(key, 102)
    mirror_seed = jax.random.fold_in(key, 103)
    key_rows = jnp.clip(jax.random.normal(key_seed, (TOKENS, HEAD), jnp.float32), -4.0, 4.0)
    query_rows = jnp.clip(jax.random.normal(query_seed, (TOKENS, QHEADS, HEAD), jnp.float32), -6.0, 6.0)
    reflect_rows = jnp.clip(jax.random.normal(mirror_seed, (TOKENS, HEAD), jnp.float32), -6.0, 6.0)
    return (query_rows.reshape(TOKENS, QHEADS * HEAD), key_rows, reflect_rows)


def draw_queries(key, part):
    return joint_draw(key)[0].astype(jnp.bfloat16)


def draw_keys(key, part):
    return joint_draw(key)[1].astype(jnp.bfloat16)


def draw_reflect(key, part):
    return joint_draw(key)[2].astype(jnp.bfloat16)


def draw_reflect_logit(key, part):
    size_seed = jax.random.fold_in(key, 201)
    sign_seed = jax.random.fold_in(key, 202)
    magnitude = jax.random.uniform(size_seed, (TOKENS,), jnp.float32, 4.0, 8.0)
    flips = jax.random.bernoulli(sign_seed, 0.5, (TOKENS,))
    return jnp.where(flips, magnitude, -magnitude).astype(jnp.float32)


def shard_levels(own_key, shape, shards, least, largest):
    factor_of, own = 1.0, jax.random.fold_in(own_key, 6)
    for dim, parts in shards:
        heights = jnp.exp(jax.random.uniform(jax.random.fold_in(own, dim), (parts,), jnp.float32, least / len(shards), largest / len(shards)))
        factor_of = factor_of * jnp.repeat(heights, shape[dim] // parts).reshape([-1 if axis == dim else 1 for axis in range(len(shape))])
    return factor_of


def length_profile(amount, total, most, skew):
    loads = [(1 << 20) // math.isqrt(grade ** skew) + 1 for grade in range(2, amount + 1)]
    spare, given = total - most - (amount - 1), [1] * (amount - 1)
    while spare > 0:
        candidates = [i for i in range(amount - 1) if given[i] < most]
        mass, left = sum([loads[i] for i in candidates]), spare
        for i in candidates:
            addition = min(most - given[i], max(1, left * loads[i] // mass), spare)
            given[i] = given[i] + addition
            spare = spare - addition
    return np.array([most] + given)


def ragged_sizes(stream_key, amount, total, most, lean):
    if amount == 2:
        one = jax.random.randint(stream_key, (), max(1, total - most), min(most, total - 1) + 1)
        return jnp.stack([one, total - one])
    tallies = jnp.asarray(length_profile(amount, total, most, lean), jnp.int32)
    pairs = (amount - 1) // 2
    source_of, sink = tallies[1:1 + 2 * pairs:2], tallies[2:2 + 2 * pairs:2]
    margin = jnp.minimum(source_of - 1, most - sink)
    moved = jax.random.randint(jax.random.fold_in(stream_key, 1), (pairs,), 0, 1 << 20) % (margin + 1)
    tallies = tallies.at[1:1 + 2 * pairs:2].set(source_of - moved).at[2:2 + 2 * pairs:2].set(sink + moved)
    return tallies[jax.random.permutation(jax.random.fold_in(stream_key, 2), amount)]


def normal_values(own_key, shape, deviation, most, split=(), kind=jnp.bfloat16):
    entries = deviation * jax.random.normal(own_key, shape, jnp.float32)
    if split:
        entries = entries * shard_levels(own_key, shape, split, -0.22, 0.18)
    return jnp.clip(entries, -most, most).astype(kind)


def setup_inputs(seed: int = 0) -> dict:
    streams_of = jax.random.split(jax.random.key(seed), 7)
    queries = draw_queries(jax.random.fold_in(streams_of[6], 71), 0)
    keys = draw_keys(jax.random.fold_in(streams_of[6], 71), 0)
    values = normal_values(streams_of[2], (TOKENS, HEAD), 1.0, 6.0, ((0, 32),))
    reflect = draw_reflect(jax.random.fold_in(streams_of[6], 71), 0)
    reflect_logit = draw_reflect_logit(jax.random.fold_in(streams_of[6], 71), 0)
    doc_of_block = jnp.searchsorted(jnp.cumsum(ragged_sizes(streams_of[5], 16, BLOCKS, MOST, 1)), jnp.arange(BLOCKS), side="right").astype(jnp.int32)
    return {"queries": queries, "keys": keys, "values": values, "reflect": reflect, "reflect_logit": reflect_logit, "doc_of_block": doc_of_block}


def matmul(left_side, right_side):
    return jnp.dot(left_side, right_side, precision=lax.Precision.HIGHEST, preferred_element_type=jnp.float32)

def apply_map(vectors, matrix):
    return lax.dot_general(vectors, matrix, (((1,), (1,)), ((), ())), precision=lax.Precision.HIGHEST, preferred_element_type=jnp.float32)

def unit_inverse(strict_part):
    length = strict_part.shape[0]
    identity = jnp.eye(length, dtype=jnp.float32)
    result = identity - strict_part
    power = strict_part
    reach = 2
    while reach < length:
        power = matmul(power, power)
        result = matmul(result, identity + power)
        reach = reach * 2
    return result

def prepare(queries, keys, reflect, reflect_logit):
    length = keys.shape[0]
    head_size = keys.shape[1]
    head_count = queries.shape[1] // head_size
    direction = reflect.astype(jnp.float32)
    direction = direction * lax.rsqrt(lax.optimization_barrier(jnp.sum(direction * direction, axis=1, keepdims=True)) + 1e-06)
    strength = 2.0 * jax.nn.sigmoid(reflect_logit.astype(jnp.float32))
    scaled_dirs = direction * strength[:, None]
    places = jnp.arange(length)
    strictly = places[:, None] > places[None, :]
    intersection = apply_map(direction, direction)
    lower_inverse = unit_inverse(jnp.where(strictly, intersection, 0.0) * strength[None, :])
    upper_inverse = unit_inverse(jnp.where(strictly.T, intersection, 0.0) * strength[None, :])
    key_float = keys.astype(jnp.float32)
    updates = matmul(lower_inverse, jnp.where(strictly, apply_map(direction, key_float), 0.0))
    key_end = key_float - matmul(updates.T, scaled_dirs)
    reflected = matmul(lower_inverse, direction)
    transit = jnp.eye(head_size, dtype=jnp.float32) - matmul(scaled_dirs.T, reflected)
    query_rows = queries.reshape(length, head_count, head_size).transpose(1, 0, 2).reshape(head_count * length, head_size)
    query_float = query_rows.astype(jnp.float32)
    facing = apply_map(query_float, direction)
    query_places = jnp.tile(places, head_count)
    visible = places[None, :] <= query_places[:, None]
    solved = matmul(upper_inverse, jnp.where(visible.T, facing.T, 0.0))
    query_turned = (query_float - matmul(solved.T, scaled_dirs)).astype(jnp.bfloat16)
    direct = lax.dot_general(query_rows, keys, (((1,), (1,)), ((), ())), preferred_element_type=jnp.float32)
    inside = (direct - matmul(jnp.where(visible, facing, 0.0) * strength[None, :], updates)) * head_size ** (-0.5)
    inside = jnp.where(visible, inside, -1e+30)
    return (query_turned, inside, key_end, transit)

def reference(queries, keys, values, reflect, reflect_logit, doc_of_block):
    head_size = keys.shape[1]
    head_count = queries.shape[1] // head_size
    stack_depth = MOST - 1

    def per_block(stacks, inputs):
        stack_keys, stack_values, stack_docs = stacks
        query_block, key_block, value_block, reflect_block, logit_block, doc_now = inputs
        query_turned, inside, key_end, transit = prepare(query_block, key_block, reflect_block, logit_block)
        flat_keys = stack_keys.reshape(stack_depth * TOK_DEV, head_size)
        remote = lax.dot_general(query_turned, flat_keys.astype(jnp.bfloat16), (((1,), (1,)), ((), ())), preferred_element_type=jnp.float32) * head_size ** (-0.5)
        allowed = jnp.repeat(stack_docs == doc_now, TOK_DEV)
        remote = jnp.where(allowed[None, :], remote, -1e+30)
        row_peak = jnp.maximum(lax.optimization_barrier(jnp.max(inside, axis=1, keepdims=True)), lax.optimization_barrier(jnp.max(remote, axis=1, keepdims=True)))
        near_w = jnp.exp(inside - row_peak)
        far_w = jnp.exp(remote - row_peak)
        weight_sum = lax.optimization_barrier(jnp.sum(near_w, axis=1, keepdims=True)) + lax.optimization_barrier(jnp.sum(far_w, axis=1, keepdims=True))
        weighted = jnp.dot(near_w.astype(jnp.bfloat16), value_block, preferred_element_type=jnp.float32)
        weighted = weighted + jnp.dot(far_w.astype(jnp.bfloat16), stack_values.reshape(stack_depth * TOK_DEV, head_size), preferred_element_type=jnp.float32)
        result = (weighted / weight_sum).reshape(head_count, TOK_DEV, head_size).transpose(1, 0, 2)
        attended_block = result.reshape(TOK_DEV, head_count * head_size).astype(jnp.bfloat16)
        carried = apply_map(flat_keys, transit).reshape(stack_depth, TOK_DEV, head_size)
        stack_keys = jnp.concatenate([carried[1:], key_end[None]], axis=0)
        stack_values = jnp.concatenate([stack_values[1:], value_block[None]], axis=0)
        stack_docs = jnp.concatenate([stack_docs[1:], doc_now[None]], axis=0)
        return ((stack_keys, stack_values, stack_docs), attended_block)
    opening = (jnp.zeros((stack_depth, TOK_DEV, head_size), jnp.float32), jnp.zeros((stack_depth, TOK_DEV, head_size), jnp.bfloat16), jnp.full((stack_depth,), -1, jnp.int32))
    inputs = (queries.reshape(BLOCKS, TOK_DEV, head_count * head_size), keys.reshape(BLOCKS, TOK_DEV, head_size), values.reshape(BLOCKS, TOK_DEV, head_size), reflect.reshape(BLOCKS, TOK_DEV, head_size), reflect_logit.reshape(BLOCKS, TOK_DEV), doc_of_block.astype(jnp.int32))
    final_stacks, blocks_out = lax.scan(per_block, opening, inputs)
    return blocks_out.reshape(TOKENS, head_count * head_size)
```

```python
import functools
import math

import jax
import jax.numpy as jnp
from jax import lax
from jax.experimental import pallas as pl
from jax.experimental.pallas import tpu as pltpu
from jax.sharding import PartitionSpec as P

F32 = jnp.float32
BF16 = jnp.bfloat16
AXES = ("outer", "inner")
GROUP = 3
VMEM_LIMIT = 48 * 1024 * 1024


def dot(left, right):
    return jnp.dot(left, right, preferred_element_type=F32)


def dot_rows(left, right):
    return lax.dot_general(left, right, (((1,), (1,)), ((), ())), preferred_element_type=F32)


def halves(value):
    high = value.astype(BF16)
    return high, (value - high.astype(F32)).astype(BF16)


def dot_halves(left, right):
    (left_high, left_low), (right_high, right_low) = left, right
    return dot(left_high, right_high) + (dot(left_high, right_low) + dot(left_low, right_high))


def unit_inverses(strict_parts):
    length = strict_parts[0].shape[0]
    rows = lax.broadcasted_iota(jnp.int32, (length, length), 0)
    columns = lax.broadcasted_iota(jnp.int32, (length, length), 1)
    identity = (rows == columns).astype(F32)
    results = [identity - part for part in strict_parts]
    powers = [halves(part) for part in strict_parts]
    reach = 2
    while reach < length:
        powers = [halves(dot_halves(power, power)) for power in powers]
        results = [
            result + dot_halves(halves(result), power) for result, power in zip(results, powers)
        ]
        reach = reach * 2
    return results


def key_kernel(reflect_ref, keys_ref, values_ref, logit_ref, packet_ref, solved_ref, gain_ref):
    reflect = reflect_ref[...]
    keys = keys_ref[...]
    length, head_size = reflect.shape
    half = length // 2
    reflect_float = reflect.astype(F32)
    square_high, square_low = halves(reflect_float * reflect_float)
    ones = jnp.ones((8, head_size), BF16)
    norms = dot_rows(ones, square_high) + dot_rows(ones, square_low)
    strength = 2.0 / (1.0 + jnp.exp(-logit_ref[...]))
    gains = strength / (norms + 1e-06)
    gain_ref[...] = gains
    gain = gains[0:1, :]
    rows = lax.broadcasted_iota(jnp.int32, (length, length), 0)
    columns = lax.broadcasted_iota(jnp.int32, (length, length), 1)
    strictly = rows > columns
    chained = jnp.where(strictly, dot_rows(reflect, reflect) * gain, 0.0)
    facing = jnp.where(strictly, dot_rows(reflect, keys), 0.0)
    reflect_turned = reflect_float.T
    keys_turned = keys.astype(F32).T
    scaled = halves(reflect_turned * gain)
    first, second = unit_inverses([chained[:half, :half], chained[half:, half:]])
    first, second = halves(first), halves(second)
    wide = jnp.concatenate([facing[:half, :half], reflect_float[:half]], axis=1)
    upper = dot_halves(first, halves(wide))
    tall = jnp.concatenate([facing[half:, :half], reflect_float[half:], facing[half:, half:]], axis=1)
    lower = dot_halves(second, halves(tall))
    bridge = dot_halves(second, halves(chained[half:, :half]))
    cross = dot_halves(halves(bridge), halves(upper))
    lower_left = lower[:, : half + head_size] - cross
    solved = jnp.concatenate(
        [
            jnp.concatenate(
                [upper[:, :half], jnp.zeros((half, half), F32), upper[:, half:]], axis=1
            ),
            jnp.concatenate(
                [lower_left[:, :half], lower[:, half + head_size :], lower_left[:, half:]], axis=1
            ),
        ],
        axis=0,
    )
    solved = halves(solved)
    wide_size = length + head_size
    solved_ref[:, :wide_size] = solved[0]
    solved_ref[:, wide_size:] = solved[1]
    change = dot_halves(scaled, solved)
    head_rows = lax.broadcasted_iota(jnp.int32, (head_size, head_size), 0)
    head_columns = lax.broadcasted_iota(jnp.int32, (head_size, head_size), 1)
    identity = (head_rows == head_columns).astype(F32)
    packet_ref[:, :length] = (keys_turned - change[:, :length]).astype(BF16)
    packet_ref[:, length:wide_size] = (identity - change[:, length:]).astype(BF16)
    for part in range(length // head_size):
        start = wide_size + part * head_size
        packet_ref[:, start : start + head_size] = values_ref[
            part * head_size : (part + 1) * head_size, :
        ]


def query_kernel(
    head_count,
    queries_ref,
    reflect_ref,
    keys_ref,
    values_ref,
    solved_ref,
    gain_ref,
    turned_ref,
    peak_ref,
    total_ref,
    weighted_ref,
):
    length, head_size = keys_ref.shape
    wide_size = length + head_size
    rate = math.log2(math.e) * head_size ** (-0.5)
    rows = lax.broadcasted_iota(jnp.int32, (length, length), 0)
    columns = lax.broadcasted_iota(jnp.int32, (length, length), 1)
    visible = rows >= columns
    gain = jnp.where(visible, gain_ref[0:1, :], 0.0)
    hidden = jnp.where(visible, 0.0, -1e30)
    both = jnp.concatenate([reflect_ref[...], keys_ref[...]], axis=0)
    solved_high = solved_ref[:, :wide_size]
    solved_low = solved_ref[:, wide_size:]
    values = values_ref[...]
    for head in range(head_count):
        span = slice(head * head_size, (head + 1) * head_size)
        queries = queries_ref[:, span]
        faced = dot_rows(queries, both)
        change = dot_halves(halves(faced[:, :length] * gain), (solved_high, solved_low))
        scores = (faced[:, length:] - change[:, :length]) + hidden
        turned_ref[:, span] = (queries.astype(F32) - change[:, length:]).astype(BF16)
        peak = jnp.max(scores, axis=1, keepdims=True)
        weights = jnp.exp2((scores - peak) * rate)
        total = jnp.sum(weights, axis=1, keepdims=True)
        weighted_ref[:, span] = dot(weights.astype(BF16), values)
        peak_ref[:, span] = jnp.broadcast_to(peak, (length, head_size))
        total_ref[:, span] = jnp.broadcast_to(total, (length, head_size))


def earlier_kernel(head_count, longest, docs_ref, *refs):
    packet_refs = refs[: longest - 1]
    turned_ref, peak_ref, total_ref, weighted_ref, out_ref, keys_ref, values_ref = refs[longest - 1 :]
    length = turned_ref.shape[0]
    head_size = turned_ref.shape[1] // head_count
    wide_size = length + head_size
    rate = math.log2(math.e) * head_size ** (-0.5)
    block = lax.axis_index("outer") * lax.axis_size("inner") + lax.axis_index("inner")
    own_doc = docs_ref[block]
    present = jnp.int32(0)
    for distance in range(1, longest):
        source = block - distance
        same = (source >= 0) & (docs_ref[jnp.maximum(source, 0)] == own_doc)
        present = present + same.astype(jnp.int32)
    odd = (block % 2) == 1
    steps = longest // 2 - 1
    apart_refs, swapped_refs, mixed_ref = (
        packet_refs[:steps],
        packet_refs[steps : 2 * steps],
        packet_refs[2 * steps],
    )
    transit = None
    for distance in range(1, longest):
        if distance % 2 == 0:
            packet = apart_refs[distance // 2 - 1][...]
        else:
            odd_ref = mixed_ref if distance == 1 else swapped_refs[(distance - 1) // 2 - 1]
            even_ref = mixed_ref if distance == longest - 1 else swapped_refs[(distance + 1) // 2 - 1]
            packet = jnp.where(odd, odd_ref[...], even_ref[...])
        keys = packet[:, :length]
        own_transit = packet[:, length:wide_size]
        slot, place = (distance - 1) // GROUP, (distance - 1) % GROUP
        if distance == 1:
            transit = own_transit.astype(F32)
        elif distance == 2:
            first = transit.astype(BF16)
            keys = dot(first, keys).astype(BF16)
            transit = dot(first, own_transit)
        else:
            high, low = halves(transit)
            keys = (dot(high, keys) + dot(low, keys)).astype(BF16)
            if distance < longest - 1:
                transit = dot(high, own_transit) + dot(low, own_transit)
        keys_ref[slot, :, place * length : (place + 1) * length] = keys
        for part in range(length // head_size):
            start = wide_size + part * head_size
            row = place * length + part * head_size
            values_ref[slot, row : row + head_size, :] = packet[:, start : start + head_size]
    slots = keys_ref.shape[0]
    for extra in range(longest - 1, slots * GROUP):
        slot, place = extra // GROUP, extra % GROUP
        keys_ref[slot, :, place * length : (place + 1) * length] = jnp.zeros(
            (head_size, length), BF16
        )
        values_ref[slot, place * length : (place + 1) * length, :] = jnp.zeros(
            (length, head_size), BF16
        )
    spot = lax.broadcasted_iota(jnp.int32, (1, GROUP * length), 1)

    def visit(slot):
        hidden = jnp.where(spot < (present - slot * GROUP) * length, 0.0, -1e30)
        keys = keys_ref[slot]
        values = values_ref[slot]
        for head in range(head_count):
            span = slice(head * head_size, (head + 1) * head_size)
            scores = dot(turned_ref[:, span], keys) + hidden
            old_peak = peak_ref[:, span][:, 0:1]
            peak = jnp.maximum(old_peak, jnp.max(scores, axis=1, keepdims=True))
            weights = jnp.exp2((scores - peak) * rate)
            factor = jnp.exp2((old_peak - peak) * rate)
            total = total_ref[:, span][:, 0:1] * factor + jnp.sum(weights, axis=1, keepdims=True)
            weighted = weighted_ref[:, span] * factor + dot(weights.astype(BF16), values)
            if slots == 1:
                out_ref[:, span] = (weighted / total).astype(BF16)
            else:
                peak_ref[:, span] = jnp.broadcast_to(peak, (length, head_size))
                total_ref[:, span] = jnp.broadcast_to(total, (length, head_size))
                weighted_ref[:, span] = weighted

    def finish():
        for head in range(head_count):
            span = slice(head * head_size, (head + 1) * head_size)
            out_ref[:, span] = (weighted_ref[:, span] / total_ref[:, span]).astype(BF16)

    if slots == 1:
        visit(0)
    else:
        @pl.loop(0, (present + GROUP - 1) // GROUP)
        def _(slot):
            visit(slot)

        finish()


def vmem(count):
    return [pl.BlockSpec(memory_space=pltpu.VMEM)] * count


def permuted(value, target):
    count = lax.axis_size("outer") * lax.axis_size("inner")
    return lax.ppermute(value, AXES, [(i, target(i) % count) for i in range(count)])


def local(queries, keys, values, reflect, reflect_logit, doc_of_block):
    longest = lax.axis_size("outer") * lax.axis_size("inner") // 8
    length, head_size = keys.shape
    head_count = queries.shape[1] // head_size
    wide_size = length + head_size
    params = pltpu.CompilerParams(vmem_limit_bytes=VMEM_LIMIT)
    packet, solved, gain = pl.pallas_call(
        key_kernel,
        out_shape=(
            jax.ShapeDtypeStruct((head_size, wide_size + length), BF16),
            jax.ShapeDtypeStruct((length, 2 * wide_size), BF16),
            jax.ShapeDtypeStruct((8, length), F32),
        ),
        in_specs=vmem(4),
        out_specs=tuple(vmem(3)),
        compiler_params=params,
        cost_estimate=pl.CostEstimate(
            flops=40 * length**3, bytes_accessed=8 * length * length, transcendentals=length
        ),
        name="key_side",
    )(reflect, keys, values, reflect_logit.reshape(1, length))
    apart = [permuted(packet, lambda i, s=s: i + 2 * s) for s in range(1, longest // 2)]
    mixed = permuted(packet, lambda i: i + longest - 1 if i % 2 else i + 1)
    swapped = [permuted(moved, lambda i: i ^ 1) for moved in apart]
    wide = jax.ShapeDtypeStruct(queries.shape, F32)
    turned, peak, total, weighted = pl.pallas_call(
        functools.partial(query_kernel, head_count),
        out_shape=(jax.ShapeDtypeStruct(queries.shape, BF16), wide, wide, wide),
        in_specs=vmem(6),
        out_specs=tuple(vmem(4)),
        compiler_params=params,
        cost_estimate=pl.CostEstimate(
            flops=head_count * 10 * length**3,
            bytes_accessed=16 * length * length * head_count,
            transcendentals=head_count * length * length,
        ),
        name="query_side",
    )(queries, reflect, keys, values, solved, gain)
    slots = (longest - 1 + GROUP - 1) // GROUP
    return pl.pallas_call(
        functools.partial(earlier_kernel, head_count, longest),
        out_shape=jax.ShapeDtypeStruct(queries.shape, BF16),
        in_specs=[pl.BlockSpec(memory_space=pltpu.SMEM)] + vmem(longest - 1 + 4),
        out_specs=vmem(1)[0],
        scratch_shapes=[
            pltpu.VMEM((slots, head_size, GROUP * length), BF16),
            pltpu.VMEM((slots, GROUP * length, head_size), BF16),
        ],
        compiler_params=params,
        cost_estimate=pl.CostEstimate(
            flops=head_count * 6 * length**3,
            bytes_accessed=16 * length * length * head_count,
            transcendentals=3 * head_count * length * length,
        ),
        name="earlier_blocks",
    )(doc_of_block, *apart, *swapped, mixed, turned, peak, total, weighted)


def solution(mesh):
    placed = (
        P(AXES, None),
        P(AXES, None),
        P(AXES, None),
        P(AXES, None),
        P(AXES),
        P(),
    )
    return jax.shard_map(
        local, mesh=mesh, in_specs=placed, out_specs=P(AXES, None), check_vma=False
    )
```

```python
import functools
import math

import jax
import jax.numpy as jnp
from jax import lax
from jax.experimental import pallas as pl
from jax.experimental.pallas import tpu as pltpu
from jax.sharding import PartitionSpec as P

F32 = jnp.float32
BF16 = jnp.bfloat16
AXES = ("outer", "inner")
GROUP = 3
VMEM_LIMIT = 48 * 1024 * 1024


def dot(left, right):
    return jnp.dot(left, right, preferred_element_type=F32)


def dot_rows(left, right):
    return lax.dot_general(left, right, (((1,), (1,)), ((), ())), preferred_element_type=F32)


def halves(value):
    high = value.astype(BF16)
    return high, (value - high.astype(F32)).astype(BF16)


def dot_halves(left, right):
    (left_high, left_low), (right_high, right_low) = left, right
    return dot(left_high, right_high) + (dot(left_high, right_low) + dot(left_low, right_high))


def unit_inverses(strict_parts):
    length = strict_parts[0].shape[0]
    rows = lax.broadcasted_iota(jnp.int32, (length, length), 0)
    columns = lax.broadcasted_iota(jnp.int32, (length, length), 1)
    identity = (rows == columns).astype(F32)
    results = [identity - part for part in strict_parts]
    powers = [halves(part) for part in strict_parts]
    reach = 2
    while reach < length:
        powers = [halves(dot_halves(power, power)) for power in powers]
        results = [
            result + dot_halves(halves(result), power) for result, power in zip(results, powers)
        ]
        reach = reach * 2
    return results


def key_kernel(
    reflect_hbm,
    keys_hbm,
    values_hbm,
    logit_hbm,
    packet_ref,
    solved_ref,
    gain_ref,
    turned_ref,
    ones_ref,
    reflect_ref,
    keys_ref,
    logit_ref,
    sems,
):
    length, head_size = reflect_ref.shape
    half = length // 2
    wide_size = length + head_size
    copies = [
        pltpu.make_async_copy(reflect_hbm, reflect_ref, sems.at[0]),
        pltpu.make_async_copy(logit_hbm, logit_ref, sems.at[1]),
        pltpu.make_async_copy(keys_hbm, keys_ref, sems.at[2]),
        pltpu.make_async_copy(values_hbm, ones_ref.at[:, pl.ds(0, head_size)], sems.at[3]),
    ]
    for copy in copies:
        copy.start()
    copies[0].wait()
    copies[1].wait()
    reflect = reflect_ref[...]
    reflect_float = reflect.astype(F32)
    square_high, square_low = halves(reflect_float * reflect_float)
    ones = jnp.ones((8, head_size), BF16)
    norms = dot_rows(ones, square_high) + dot_rows(ones, square_low)
    strength = 2.0 / (1.0 + jnp.exp(-logit_ref[...]))
    gains = strength / (norms + 1e-06)
    gain_ref[...] = gains
    gain = gains[0:1, :]
    rows = lax.broadcasted_iota(jnp.int32, (length, length), 0)
    columns = lax.broadcasted_iota(jnp.int32, (length, length), 1)
    strictly = rows > columns
    chained = jnp.where(strictly, dot_rows(reflect, reflect) * gain, 0.0)
    reflect_turned = reflect_float.T
    copies[2].wait()
    keys = keys_ref[...]
    facing = jnp.where(strictly, dot_rows(reflect, keys), 0.0)
    keys_turned = keys.astype(F32).T
    turned_ref[:, :length] = reflect_turned.astype(BF16)
    turned_ref[:, length:] = keys_turned.astype(BF16)
    scaled = halves(reflect_turned * gain)
    first, second = unit_inverses([chained[:half, :half], chained[half:, half:]])
    first, second = halves(first), halves(second)
    wide = jnp.concatenate([facing[:half, :half], reflect_float[:half]], axis=1)
    upper = dot_halves(first, halves(wide))
    tall = jnp.concatenate([facing[half:, :half], reflect_float[half:], facing[half:, half:]], axis=1)
    lower = dot_halves(second, halves(tall))
    bridge = dot_halves(second, halves(chained[half:, :half]))
    cross = dot_halves(halves(bridge), halves(upper))
    lower_left = lower[:, : half + head_size] - cross
    solved = jnp.concatenate(
        [
            jnp.concatenate(
                [upper[:, :half], jnp.zeros((half, half), F32), upper[:, half:]], axis=1
            ),
            jnp.concatenate(
                [lower_left[:, :half], lower[:, half + head_size :], lower_left[:, half:]], axis=1
            ),
        ],
        axis=0,
    )
    solved = halves(solved)
    solved_ref[:, :wide_size] = solved[0]
    solved_ref[:, wide_size:] = solved[1]
    change = dot_halves(scaled, solved)
    head_rows = lax.broadcasted_iota(jnp.int32, (head_size, head_size), 0)
    head_columns = lax.broadcasted_iota(jnp.int32, (head_size, head_size), 1)
    identity = (head_rows == head_columns).astype(F32)
    packet_ref[:, :length] = (keys_turned - change[:, :length]).astype(BF16)
    packet_ref[:, length:wide_size] = (identity - change[:, length:]).astype(BF16)
    copies[3].wait()
    ones_ref[:, head_size:] = jnp.ones((length, head_size), BF16)
    for part in range(length // head_size):
        start = wide_size + part * head_size
        packet_ref[:, start : start + head_size] = ones_ref[
            part * head_size : (part + 1) * head_size, :head_size
        ]


def row_peak(scores, peak):
    size = peak.shape[1]
    pieces = [scores[:, i : i + size] for i in range(0, scores.shape[1], size)]
    return jnp.maximum(peak, jnp.max(functools.reduce(jnp.maximum, pieces), axis=1, keepdims=True))


def row_weights(scores, peak, rate):
    size = peak.shape[1]
    pieces = [
        jnp.exp2((scores[:, i : i + size] - peak) * rate) for i in range(0, scores.shape[1], size)
    ]
    return jnp.concatenate(pieces, axis=1).astype(BF16)


def query_kernel(
    head_count,
    longest,
    docs_hbm,
    queries_ref,
    both_ref,
    ones_ref,
    solved_ref,
    gain_ref,
    turned_ref,
    peak_ref,
    total_ref,
    weighted_ref,
    present_ref,
    docs_ref,
    docs_sem,
):
    docs_copy = pltpu.make_async_copy(docs_hbm, docs_ref, docs_sem)
    docs_copy.start()
    length = ones_ref.shape[0]
    head_size = ones_ref.shape[1] // 2
    wide_size = length + head_size
    rate = math.log2(math.e) * head_size ** (-0.5)
    rows = lax.broadcasted_iota(jnp.int32, (length, length), 0)
    columns = lax.broadcasted_iota(jnp.int32, (length, length), 1)
    visible = rows >= columns
    gain = jnp.where(visible, gain_ref[0:1, :], 0.0)
    hidden = jnp.where(visible, 0.0, -1e30)
    both = both_ref[...]
    solved_high = solved_ref[:, :wide_size]
    solved_low = solved_ref[:, wide_size:]
    values = ones_ref[...]
    for head in range(head_count):
        span = slice(head * head_size, (head + 1) * head_size)
        queries = queries_ref[:, span]
        faced = dot(queries, both)
        change = dot_halves(halves(faced[:, :length] * gain), (solved_high, solved_low))
        scores = (faced[:, length:] - change[:, :length]) + hidden
        turned_ref[:, span] = (queries.astype(F32) - change[:, length:]).astype(BF16)
        peak = jnp.broadcast_to(jnp.max(scores, axis=1, keepdims=True), (length, head_size))
        sums = dot(row_weights(scores, peak, rate), values)
        peak_ref[:, span] = peak
        weighted_ref[:, span] = sums[:, :head_size]
        total_ref[:, span] = sums[:, head_size:]
    docs_copy.wait()
    block = lax.axis_index("outer") * lax.axis_size("inner") + lax.axis_index("inner")
    own_doc = docs_ref[block]
    present = jnp.int32(0)
    for distance in range(1, longest):
        source = block - distance
        same = (source >= 0) & (docs_ref[jnp.maximum(source, 0)] == own_doc)
        present = present + same.astype(jnp.int32)
    present_ref[...] = jnp.full(present_ref.shape, present, jnp.int32)


def earlier_kernel(head_count, longest, present_ref, *refs):
    packet_refs = refs[: longest - 1]
    turned_ref, peak_ref, total_ref, weighted_ref, out_ref, keys_ref, values_ref = refs[longest - 1 :]
    length = turned_ref.shape[0]
    head_size = turned_ref.shape[1] // head_count
    wide_size = length + head_size
    rate = math.log2(math.e) * head_size ** (-0.5)
    present = jnp.max(present_ref[...])
    odd = (lax.axis_index("inner") % 2) == 1
    steps = longest // 2 - 1
    apart_refs, swapped_refs, mixed_ref = (
        packet_refs[:steps],
        packet_refs[steps : 2 * steps],
        packet_refs[2 * steps],
    )
    slots = keys_ref.shape[0]

    def gather():
        transit = None
        for distance in range(1, longest):
            if distance % 2 == 0:
                packet = apart_refs[distance // 2 - 1][...]
            else:
                odd_ref = mixed_ref if distance == 1 else swapped_refs[(distance - 1) // 2 - 1]
                even_ref = (
                    mixed_ref if distance == longest - 1 else swapped_refs[(distance + 1) // 2 - 1]
                )
                packet = jnp.where(odd, odd_ref[...], even_ref[...])
            keys = packet[:, :length]
            own_transit = packet[:, length:wide_size]
            slot, place = (distance - 1) // GROUP, (distance - 1) % GROUP
            if distance == 1:
                transit = own_transit
            elif distance == 2:
                keys = dot(transit, keys).astype(BF16)
                transit = dot(transit, own_transit)
            else:
                high, low = halves(transit)
                keys = (dot(high, keys) + dot(low, keys)).astype(BF16)
                if distance < longest - 1:
                    transit = dot(high, own_transit) + dot(low, own_transit)
            keys_ref[slot, :, place * length : (place + 1) * length] = keys
            for part in range(length // head_size):
                start = wide_size + part * head_size
                row = place * length + part * head_size
                values_ref[slot, row : row + head_size, :head_size] = packet[
                    :, start : start + head_size
                ]
        for slot in range(slots):
            values_ref[slot, :, head_size:] = jnp.ones((GROUP * length, head_size), BF16)

    def visit(slot, blocks):
        keys = keys_ref[slot, :, : blocks * length]
        values = values_ref[slot, : blocks * length, :]
        for head in range(head_count):
            span = slice(head * head_size, (head + 1) * head_size)
            scores = dot(turned_ref[:, span], keys)
            old_peak = peak_ref[:, span]
            peak = row_peak(scores, old_peak)
            sums = dot(row_weights(scores, peak, rate), values)
            factor = jnp.exp2((old_peak - peak) * rate)
            total = total_ref[:, span] * factor + sums[:, head_size:]
            weighted = weighted_ref[:, span] * factor + sums[:, :head_size]
            if slots == 1:
                out_ref[:, span] = (weighted / total).astype(BF16)
            else:
                peak_ref[:, span] = peak
                total_ref[:, span] = total
                weighted_ref[:, span] = weighted

    def finish():
        for head in range(head_count):
            span = slice(head * head_size, (head + 1) * head_size)
            out_ref[:, span] = (weighted_ref[:, span] / total_ref[:, span]).astype(BF16)

    @pl.when(present > 0)
    def _():
        gather()

    if slots == 1:
        pl.when(present == 0)(finish)
        for blocks in range(1, longest):
            pl.when(present == blocks)(functools.partial(visit, 0, blocks))
    else:
        full = present // GROUP

        @pl.loop(0, full)
        def _(slot):
            visit(slot, GROUP)

        for blocks in range(1, GROUP):
            pl.when(present % GROUP == blocks)(functools.partial(visit, full, blocks))
        finish()


def vmem(count):
    return [pl.BlockSpec(memory_space=pltpu.VMEM)] * count


def in_hbm(value):
    return pltpu.with_memory_space_constraint(value, pltpu.HBM)


def permuted(value, target):
    count = lax.axis_size("outer") * lax.axis_size("inner")
    return lax.ppermute(value, AXES, [(i, target(i) % count) for i in range(count)])


def local(queries, keys, values, reflect, reflect_logit, doc_of_block):
    longest = lax.axis_size("outer") * lax.axis_size("inner") // 8
    length, head_size = keys.shape
    head_count = queries.shape[1] // head_size
    wide_size = length + head_size
    params = pltpu.CompilerParams(vmem_limit_bytes=VMEM_LIMIT)
    shape = jax.ShapeDtypeStruct
    hbm = pl.BlockSpec(memory_space=pltpu.HBM)
    packet, solved, gain, both, ones = pl.pallas_call(
        key_kernel,
        out_shape=(
            shape((head_size, wide_size + length), BF16),
            shape((length, 2 * wide_size), BF16),
            shape((8, length), F32),
            shape((head_size, 2 * length), BF16),
            shape((length, 2 * head_size), BF16),
        ),
        in_specs=[hbm] * 4,
        out_specs=tuple(vmem(5)),
        scratch_shapes=[
            pltpu.VMEM((length, head_size), BF16),
            pltpu.VMEM((length, head_size), BF16),
            pltpu.VMEM((1, length), F32),
            pltpu.SemaphoreType.DMA((4,)),
        ],
        compiler_params=params,
        cost_estimate=pl.CostEstimate(
            flops=40 * length**3, bytes_accessed=8 * length * length, transcendentals=length
        ),
        name="key_side",
    )(*(in_hbm(value) for value in (reflect, keys, values, reflect_logit.reshape(1, length))))
    apart = [permuted(packet, lambda i, s=s: i + 2 * s) for s in range(1, longest // 2)]
    mixed = permuted(packet, lambda i: i + longest - 1 if i % 2 else i + 1)
    wide = shape(queries.shape, F32)
    turned, peak, total, weighted, present = pl.pallas_call(
        functools.partial(query_kernel, head_count, longest),
        out_shape=(shape(queries.shape, BF16), wide, wide, wide, shape((8, 128), jnp.int32)),
        in_specs=[hbm] + vmem(5),
        out_specs=tuple(vmem(5)),
        scratch_shapes=[
            pltpu.SMEM(doc_of_block.shape, jnp.int32),
            pltpu.SemaphoreType.DMA(()),
        ],
        compiler_params=params,
        cost_estimate=pl.CostEstimate(
            flops=head_count * 10 * length**3,
            bytes_accessed=16 * length * length * head_count,
            transcendentals=head_count * length * length,
        ),
        name="query_side",
    )(in_hbm(doc_of_block), queries, both, ones, solved, gain)
    *apart, turned = lax.optimization_barrier((*apart, turned))
    swapped = [permuted(moved, lambda i: i ^ 1) for moved in apart]
    slots = (longest - 1 + GROUP - 1) // GROUP
    return pl.pallas_call(
        functools.partial(earlier_kernel, head_count, longest),
        out_shape=shape(queries.shape, BF16),
        in_specs=vmem(longest - 1 + 5),
        out_specs=vmem(1)[0],
        scratch_shapes=[
            pltpu.VMEM((slots, head_size, GROUP * length), BF16),
            pltpu.VMEM((slots, GROUP * length, 2 * head_size), BF16),
        ],
        compiler_params=params,
        cost_estimate=pl.CostEstimate(
            flops=head_count * 6 * length**3,
            bytes_accessed=16 * length * length * head_count,
            transcendentals=3 * head_count * length * length,
        ),
        name="earlier_blocks",
    )(present, *apart, *swapped, mixed, turned, peak, total, weighted)


def solution(mesh):
    placed = (
        P(AXES, None),
        P(AXES, None),
        P(AXES, None),
        P(AXES, None),
        P(AXES),
        P(),
    )
    return jax.shard_map(
        local, mesh=mesh, in_specs=placed, out_specs=P(AXES, None), check_vma=False
    )
```

```python
import functools
import math

import jax
import jax.numpy as jnp
from jax import lax
from jax.experimental import pallas as pl
from jax.experimental.pallas import tpu as pltpu
from jax.sharding import PartitionSpec as P

F32 = jnp.float32
BF16 = jnp.bfloat16
AXES = ("outer", "inner")
GROUP = 3
VMEM_LIMIT = 24 * 1024 * 1024


def dot(left, right):
    return jnp.dot(left, right, preferred_element_type=F32)


def dot_rows(left, right):
    return lax.dot_general(left, right, (((1,), (1,)), ((), ())), preferred_element_type=F32)


def halves(value):
    high = value.astype(BF16)
    return high, (value - high.astype(F32)).astype(BF16)


def dot_halves(left, right):
    (left_high, left_low), (right_high, right_low) = left, right
    return dot(left_high, right_high) + (dot(left_high, right_low) + dot(left_low, right_high))


def unit_inverses(strict_parts):
    length = strict_parts[0].shape[0]
    rows = lax.broadcasted_iota(jnp.int32, (length, length), 0)
    columns = lax.broadcasted_iota(jnp.int32, (length, length), 1)
    identity = (rows == columns).astype(F32)
    results = [identity - part for part in strict_parts]
    powers = [halves(part) for part in strict_parts]
    reach = 2
    while reach < length:
        powers = [halves(dot_halves(power, power)) for power in powers]
        results = [
            result + dot_halves(halves(result), power) for result, power in zip(results, powers)
        ]
        reach = reach * 2
    return results


def key_kernel(
    reflect_hbm,
    keys_hbm,
    values_hbm,
    logit_hbm,
    packet_ref,
    solved_ref,
    gain_ref,
    turned_ref,
    ones_ref,
    reflect_ref,
    keys_ref,
    logit_ref,
    sems,
):
    length, head_size = reflect_ref.shape
    half = length // 2
    wide_size = length + head_size
    copies = [
        pltpu.make_async_copy(reflect_hbm, reflect_ref, sems.at[0]),
        pltpu.make_async_copy(logit_hbm, logit_ref, sems.at[1]),
        pltpu.make_async_copy(keys_hbm, keys_ref, sems.at[2]),
        pltpu.make_async_copy(values_hbm, ones_ref.at[:, pl.ds(0, head_size)], sems.at[3]),
    ]
    for copy in copies:
        copy.start()
    copies[0].wait()
    copies[1].wait()
    reflect = reflect_ref[...]
    reflect_float = reflect.astype(F32)
    square_high, square_low = halves(reflect_float * reflect_float)
    ones = jnp.ones((8, head_size), BF16)
    norms = dot_rows(ones, square_high) + dot_rows(ones, square_low)
    strength = 2.0 / (1.0 + jnp.exp(-logit_ref[...]))
    gains = strength / (norms + 1e-06)
    gain_ref[...] = gains
    gain = gains[0:1, :]
    rows = lax.broadcasted_iota(jnp.int32, (length, length), 0)
    columns = lax.broadcasted_iota(jnp.int32, (length, length), 1)
    strictly = rows > columns
    chained = jnp.where(strictly, dot_rows(reflect, reflect) * gain, 0.0)
    reflect_turned = reflect_float.T
    copies[2].wait()
    keys = keys_ref[...]
    facing = jnp.where(strictly, dot_rows(reflect, keys), 0.0)
    keys_turned = keys.astype(F32).T
    turned_ref[:, :length] = reflect_turned.astype(BF16)
    turned_ref[:, length:] = keys_turned.astype(BF16)
    scaled = halves(reflect_turned * gain)
    first, second = unit_inverses([chained[:half, :half], chained[half:, half:]])
    first, second = halves(first), halves(second)
    wide = jnp.concatenate([facing[:half, :half], reflect_float[:half]], axis=1)
    upper = dot_halves(first, halves(wide))
    tall = jnp.concatenate([facing[half:, :half], reflect_float[half:], facing[half:, half:]], axis=1)
    lower = dot_halves(second, halves(tall))
    bridge = dot_halves(second, halves(chained[half:, :half]))
    cross = dot_halves(halves(bridge), halves(upper))
    lower_left = lower[:, : half + head_size] - cross
    solved = jnp.concatenate(
        [
            jnp.concatenate(
                [upper[:, :half], jnp.zeros((half, half), F32), upper[:, half:]], axis=1
            ),
            jnp.concatenate(
                [lower_left[:, :half], lower[:, half + head_size :], lower_left[:, half:]], axis=1
            ),
        ],
        axis=0,
    )
    solved = halves(solved)
    solved_ref[:, :wide_size] = solved[0]
    solved_ref[:, wide_size:] = solved[1]
    change = dot_halves(scaled, solved)
    head_rows = lax.broadcasted_iota(jnp.int32, (head_size, head_size), 0)
    head_columns = lax.broadcasted_iota(jnp.int32, (head_size, head_size), 1)
    identity = (head_rows == head_columns).astype(F32)
    packet_ref[:, :length] = (keys_turned - change[:, :length]).astype(BF16)
    packet_ref[:, length:wide_size] = (identity - change[:, length:]).astype(BF16)
    copies[3].wait()
    ones_ref[:, head_size:] = jnp.ones((length, head_size), BF16)
    for part in range(length // head_size):
        start = wide_size + part * head_size
        packet_ref[:, start : start + head_size] = ones_ref[
            part * head_size : (part + 1) * head_size, :head_size
        ]


def lane_pieces(scores, size):
    return [score[:, i : i + size] for score in scores for i in range(0, score.shape[1], size)]


def row_peak(scores, peak):
    largest = functools.reduce(jnp.maximum, lane_pieces(scores, peak.shape[1]))
    return jnp.maximum(peak, jnp.max(largest, axis=1, keepdims=True))


def row_weights(scores, peak, rate):
    pieces = [jnp.exp2((piece - peak) * rate) for piece in lane_pieces(scores, peak.shape[1])]
    return jnp.concatenate(pieces, axis=1).astype(BF16)


def reciprocal(value):
    rough = pl.reciprocal(value, approx=True)
    return rough * (2.0 - value * rough)


def query_kernel(heads, longest, *refs):
    docs_hbm, queries_ref, both_ref, ones_ref, solved_ref, gain_ref = refs[:6]
    turned_ref, peak_ref, total_ref, weighted_ref, present_ref, docs_ref, docs_sem = refs[-7:]
    if docs_hbm is not None:
        docs_copy = pltpu.make_async_copy(docs_hbm, docs_ref, docs_sem)
        docs_copy.start()
    length = ones_ref.shape[0]
    head_size = ones_ref.shape[1] // 2
    wide_size = length + head_size
    rate = math.log2(math.e) * head_size ** (-0.5)
    rows = lax.broadcasted_iota(jnp.int32, (length, length), 0)
    columns = lax.broadcasted_iota(jnp.int32, (length, length), 1)
    visible = rows >= columns
    gain = jnp.where(visible, gain_ref[0:1, :], 0.0)
    hidden = jnp.where(visible, 0.0, -1e30)
    both = both_ref[...]
    solved_high = solved_ref[:, :wide_size]
    solved_low = solved_ref[:, wide_size:]
    values = ones_ref[...]
    for head in heads:
        span = slice(head * head_size, (head + 1) * head_size)
        queries = queries_ref[:, span]
        faced = dot(queries, both)
        change = dot_halves(halves(faced[:, :length] * gain), (solved_high, solved_low))
        scores = (faced[:, length:] - change[:, :length]) + hidden
        turned_ref[:, span] = (queries.astype(F32) - change[:, length:]).astype(BF16)
        peak = jnp.broadcast_to(jnp.max(scores, axis=1, keepdims=True), (length, head_size))
        sums = dot(row_weights([scores], peak, rate), values)
        peak_ref[:, span] = peak
        weighted_ref[:, span] = sums[:, :head_size]
        total_ref[:, span] = sums[:, head_size:]
    if docs_hbm is not None:
        docs_copy.wait()
        block = lax.axis_index("outer") * lax.axis_size("inner") + lax.axis_index("inner")
        own_doc = docs_ref[block]
        present = jnp.int32(0)
        for distance in range(1, longest):
            source = block - distance
            same = (source >= 0) & (docs_ref[jnp.maximum(source, 0)] == own_doc)
            present = present + same.astype(jnp.int32)
        present_ref[...] = jnp.full(present_ref.shape, present, jnp.int32)


def other_queries(heads, longest, *refs):
    for done_ref, state_ref in zip(refs[5:9], refs[9:13]):
        state_ref[:, : done_ref.shape[1]] = done_ref[...]
    query_kernel(heads, longest, None, *refs, None, None, None)


def is_odd():
    return (lax.axis_index("inner") % 2) == 1


def put_out(out_ref, out_hbm, out_sems, head, head_size):
    span = slice(head * head_size, (head + 1) * head_size)
    return pltpu.make_async_copy(out_ref.at[:, span], out_hbm.at[:, span], out_sems.at[head])


def attend(head_count, state_refs, new_refs, all_keys, values, out_refs):
    turned_ref, peak_ref, total_ref, weighted_ref = state_refs
    head_size = turned_ref.shape[1] // head_count
    rate = math.log2(math.e) * head_size ** (-0.5)
    for head in range(head_count):
        span = slice(head * head_size, (head + 1) * head_size)
        old_peak = peak_ref[:, span]
        scores = [dot(turned_ref[:, span], keys) for keys in all_keys]
        peak = row_peak(scores, old_peak)
        sums = dot(row_weights(scores, peak, rate), values)
        factor = jnp.exp2((old_peak - peak) * rate)
        total = total_ref[:, span] * factor + sums[:, head_size:]
        weighted = weighted_ref[:, span] * factor + sums[:, :head_size]
        if out_refs is not None:
            out_refs[0][:, span] = (weighted * reciprocal(total)).astype(BF16)
            put_out(*out_refs, head, head_size).start()
        else:
            for new_ref, new in zip(new_refs, (peak, total, weighted)):
                new_ref[:, span] = new
    if out_refs is not None:
        wait_out(head_count, out_refs)


def finish(head_count, sum_refs, out_refs):
    total_ref, weighted_ref = sum_refs
    head_size = total_ref.shape[1] // head_count
    for head in range(head_count):
        span = slice(head * head_size, (head + 1) * head_size)
        out_refs[0][:, span] = (weighted_ref[:, span] * reciprocal(total_ref[:, span])).astype(BF16)
        put_out(*out_refs, head, head_size).start()
    wait_out(head_count, out_refs)


def wait_out(head_count, out_refs):
    head_size = out_refs[0].shape[1] // head_count
    for head in range(head_count):
        put_out(*out_refs, head, head_size).wait()


def store_values(values_ref, slot, place, packet, length):
    head_size = packet.shape[0]
    rows = pl.ds(place * length, length)
    start = length + head_size
    pieces = [
        packet[:, at : at + head_size] for at in range(start, start + length, head_size)
    ]
    values_ref[slot, rows, :head_size] = jnp.concatenate(pieces, axis=0)
    values_ref[slot, rows, head_size:] = jnp.ones((length, head_size), BF16)


def nearest_kernel(head_count, present_ref, mixed_ref, *refs):
    old_refs, new_refs = refs[:4], refs[4:7]
    out_hbm, out_ref, values_ref, out_sems = refs[7:]
    out_refs = (out_ref, out_hbm, out_sems)
    length = out_ref.shape[0]
    present = jnp.max(present_ref[...])
    odd = is_odd()

    def nearest(out):
        packet = mixed_ref[...]
        store_values(values_ref, 0, 0, packet, length)
        attend(head_count, old_refs, new_refs, [packet[:, :length]], values_ref[0], out)

    @pl.when(present == 0)
    def _():
        finish(head_count, old_refs[2:], out_refs)

    pl.when(odd & (present == 1))(lambda: nearest(out_refs))
    pl.when(odd & (present > 1))(lambda: nearest(None))

    @pl.when(jnp.logical_not(odd) & (present > 0))
    def _():
        for old_ref, new_ref in zip(old_refs[1:], new_refs):
            new_ref[...] = old_ref[...]


def earlier_kernel(head_count, longest, present_ref, *refs):
    packet_refs = refs[: longest - 1]
    state_refs = refs[longest - 1 : longest + 3]
    out_hbm, out_ref, keys_ref, values_ref, out_sems = refs[-5:]
    out_refs = (out_ref, out_hbm, out_sems)
    present = jnp.max(present_ref[...])
    length = out_ref.shape[0]
    head_size = out_ref.shape[1] // head_count
    wide_size = length + head_size
    odd = is_odd()
    steps = longest // 2 - 1
    apart_refs, swapped_refs, mixed_ref = (
        packet_refs[:steps],
        packet_refs[steps : 2 * steps],
        packet_refs[2 * steps],
    )
    slots = values_ref.shape[0]

    def packet_of(distance, known_odd):
        if distance % 2 == 0:
            return apart_refs[distance // 2 - 1][...]
        odd_ref = mixed_ref if distance == 1 else swapped_refs[(distance - 1) // 2 - 1]
        even_ref = mixed_ref if distance == longest - 1 else swapped_refs[(distance + 1) // 2 - 1]
        if known_odd is None:
            return jnp.where(odd, odd_ref[...], even_ref[...])
        return (odd_ref if known_odd else even_ref)[...]

    def collect(first, last, known_odd=None):
        transit = None
        all_keys = []
        for distance in range(1, last + 1):
            packet = packet_of(distance, known_odd)
            keys = packet[:, :length]
            own_transit = packet[:, length:wide_size]
            if distance == 1:
                transit = own_transit
            elif distance == 2:
                keys = dot(transit, keys).astype(BF16)
                if distance < last:
                    transit = dot(transit, own_transit)
            else:
                high, low = halves(transit)
                keys = (dot(high, keys) + dot(low, keys)).astype(BF16)
                if distance < last:
                    transit = dot(high, own_transit) + dot(low, own_transit)
            if distance >= first:
                all_keys.append(keys)
                index = distance - first
                store_values(values_ref, index // GROUP, index % GROUP, packet, length)
        return all_keys

    if slots == 1:
        for known_odd in (False, True):
            first = 2 if known_odd else 1
            for last in range(first, longest):

                @pl.when((odd == known_odd) & (present == last))
                def _(known_odd=known_odd, first=first, last=last):
                    keys = collect(first, last, known_odd)
                    values = values_ref[0, : len(keys) * length, :]
                    attend(head_count, state_refs, None, keys, values, out_refs)

    else:

        @pl.when(present > 0)
        def _():
            for index, keys in enumerate(collect(1, longest - 1)):
                slot, place = index // GROUP, index % GROUP
                keys_ref[slot, :, place * length : (place + 1) * length] = keys

        def visit(slot, blocks):
            keys = [keys_ref[slot, :, i * length : (i + 1) * length] for i in range(blocks)]
            values = values_ref[slot, : blocks * length, :]
            attend(head_count, state_refs, state_refs[1:], keys, values, None)

        full = present // GROUP

        @pl.loop(0, full)
        def _(slot):
            visit(slot, GROUP)

        for blocks in range(1, GROUP):
            pl.when(present % GROUP == blocks)(functools.partial(visit, full, blocks))
        finish(head_count, state_refs[2:], out_refs)


def vmem(count):
    return [pl.BlockSpec(memory_space=pltpu.VMEM)] * count


def in_hbm(value):
    return pltpu.with_memory_space_constraint(value, pltpu.HBM)


def permuted(value, target):
    count = lax.axis_size("outer") * lax.axis_size("inner")
    return lax.ppermute(value, AXES, [(i, target(i) % count) for i in range(count)])


def local(queries, keys, values, reflect, reflect_logit, doc_of_block):
    longest = lax.axis_size("outer") * lax.axis_size("inner") // 8
    length, head_size = keys.shape
    head_count = queries.shape[1] // head_size
    wide_size = length + head_size
    params = pltpu.CompilerParams(vmem_limit_bytes=VMEM_LIMIT)
    shape = jax.ShapeDtypeStruct
    hbm = pl.BlockSpec(memory_space=pltpu.HBM)
    packet, solved, gain, both, ones = pl.pallas_call(
        key_kernel,
        out_shape=(
            shape((head_size, wide_size + length), BF16),
            shape((length, 2 * wide_size), BF16),
            shape((8, length), F32),
            shape((head_size, 2 * length), BF16),
            shape((length, 2 * head_size), BF16),
        ),
        in_specs=[hbm] * 4,
        out_specs=tuple(vmem(5)),
        scratch_shapes=[
            pltpu.VMEM((length, head_size), BF16),
            pltpu.VMEM((length, head_size), BF16),
            pltpu.VMEM((1, length), F32),
            pltpu.SemaphoreType.DMA((4,)),
        ],
        compiler_params=params,
        cost_estimate=pl.CostEstimate(
            flops=40 * length**3, bytes_accessed=8 * length * length, transcendentals=length
        ),
        name="key_side",
    )(*(in_hbm(value) for value in (reflect, keys, values, reflect_logit.reshape(1, length))))
    apart = [permuted(packet, lambda i, s=s: i + 2 * s) for s in range(1, longest // 2)]
    wide = shape(queries.shape, F32)
    state_shapes = (shape(queries.shape, BF16), wide, wide, wide)
    first = max(1, head_count // 4)
    first_shapes = [shape((length, first * head_size), part.dtype) for part in state_shapes]

    def query_cost(heads):
        return pl.CostEstimate(
            flops=heads * 10 * length**3,
            bytes_accessed=16 * length * length * heads,
            transcendentals=heads * length * length,
        )

    *state, present = pl.pallas_call(
        functools.partial(query_kernel, range(first), longest),
        out_shape=(*first_shapes, shape((8, 128), jnp.int32)),
        in_specs=[hbm] + vmem(5),
        out_specs=tuple(vmem(5)),
        scratch_shapes=[
            pltpu.SMEM(doc_of_block.shape, jnp.int32),
            pltpu.SemaphoreType.DMA(()),
        ],
        compiler_params=params,
        cost_estimate=query_cost(first),
        name="first_queries",
    )(in_hbm(doc_of_block), queries, both, ones, solved, gain)
    mixed_packet, state[0] = lax.optimization_barrier((packet, state[0]))
    mixed = permuted(mixed_packet, lambda i: i + longest - 1 if i % 2 else i + 1)
    state = pl.pallas_call(
        functools.partial(other_queries, range(first, head_count), longest),
        out_shape=state_shapes,
        in_specs=vmem(9),
        out_specs=tuple(vmem(4)),
        compiler_params=params,
        cost_estimate=query_cost(head_count - first),
        name="other_queries",
    )(queries, both, ones, solved, gain, *state)
    *apart, turned = lax.optimization_barrier((*apart, state[0]))
    state = [turned, *state[1:]]
    swapped = [permuted(moved, lambda i: i ^ 1) for moved in apart]
    out_shape = shape(queries.shape, BF16)
    slots = (longest - 1 + GROUP - 1) // GROUP
    out_scratch = [pltpu.VMEM(queries.shape, BF16), pltpu.SemaphoreType.DMA((head_count,))]
    sums, started = state[1:], []
    if slots == 1:
        *sums, out = pl.pallas_call(
            functools.partial(nearest_kernel, head_count),
            out_shape=(*state_shapes[1:], out_shape),
            in_specs=vmem(6),
            out_specs=(*vmem(3), hbm),
            scratch_shapes=[
                out_scratch[0],
                pltpu.VMEM((1, length, 2 * head_size), BF16),
                out_scratch[1],
            ],
            compiler_params=params,
            cost_estimate=pl.CostEstimate(
                flops=head_count * 2 * length**3,
                bytes_accessed=4 * length * length * head_count,
                transcendentals=head_count * length * length,
            ),
            name="nearest_block",
        )(present, mixed, *state)
        started = [in_hbm(out)]
    return pl.pallas_call(
        functools.partial(earlier_kernel, head_count, longest),
        out_shape=out_shape,
        in_specs=vmem(longest - 1 + 5) + [hbm] * len(started),
        out_specs=hbm,
        input_output_aliases={longest + 4: 0} if started else {},
        scratch_shapes=[
            out_scratch[0],
            pltpu.VMEM((slots, head_size, GROUP * length), BF16),
            pltpu.VMEM((slots, GROUP * length, 2 * head_size), BF16),
            out_scratch[1],
        ],
        compiler_params=params,
        cost_estimate=pl.CostEstimate(
            flops=head_count * 6 * length**3,
            bytes_accessed=16 * length * length * head_count,
            transcendentals=3 * head_count * length * length,
        ),
        name="earlier_blocks",
    )(present, *apart, *swapped, mixed, turned, *sums, *started)


def solution(mesh):
    placed = (
        P(AXES, None),
        P(AXES, None),
        P(AXES, None),
        P(AXES, None),
        P(AXES),
        P(),
    )
    return jax.shard_map(
        local, mesh=mesh, in_specs=placed, out_specs=P(AXES, None), check_vma=False
    )
```

```python
import functools
import math

import jax
import jax.numpy as jnp
from jax import lax
from jax.experimental import pallas as pl
from jax.experimental.pallas import tpu as pltpu
from jax.sharding import PartitionSpec as P

F32 = jnp.float32
BF16 = jnp.bfloat16
AXES = ("outer", "inner")
GROUP = 3
VMEM_LIMIT = 24 * 1024 * 1024


def dot(left, right):
    return jnp.dot(left, right, preferred_element_type=F32)


def dot_rows(left, right):
    return lax.dot_general(left, right, (((1,), (1,)), ((), ())), preferred_element_type=F32)


def halves(value):
    high = value.astype(BF16)
    return high, (value - high.astype(F32)).astype(BF16)


def dot_halves(left, right):
    (left_high, left_low), (right_high, right_low) = left, right
    return dot(left_high, right_high) + (dot(left_high, right_low) + dot(left_low, right_high))


def unit_inverses(strict_parts):
    length = strict_parts[0].shape[0]
    rows = lax.broadcasted_iota(jnp.int32, (length, length), 0)
    columns = lax.broadcasted_iota(jnp.int32, (length, length), 1)
    identity = (rows == columns).astype(F32)
    results = [identity - part for part in strict_parts]
    powers = [halves(part) for part in strict_parts]
    powers = [dot_halves(power, power) for power in powers]
    reach = 4
    while reach < length:
        for index, (result, power) in enumerate(zip(results, powers)):
            high, low = halves(jnp.concatenate([power, result], axis=0))
            weights = (high[:length], low[:length])
            product = dot_halves((high, low), weights)
            powers[index] = product[:length]
            results[index] = result + product[length:]
        reach = reach * 2
    return [
        result + dot_halves(halves(result), halves(power))
        for result, power in zip(results, powers)
    ]


def key_kernel(
    reflect_hbm,
    keys_hbm,
    values_hbm,
    logit_hbm,
    packet_ref,
    partial_ref,
    gain_ref,
    turned_ref,
    ones_ref,
    reflect_ref,
    keys_ref,
    logit_ref,
    sems,
):
    length, head_size = reflect_ref.shape
    half = length // 2
    wide_size = length + head_size
    copies = [
        pltpu.make_async_copy(reflect_hbm, reflect_ref, sems.at[0]),
        pltpu.make_async_copy(logit_hbm, logit_ref, sems.at[1]),
        pltpu.make_async_copy(keys_hbm, keys_ref, sems.at[2]),
        pltpu.make_async_copy(values_hbm, ones_ref.at[:, pl.ds(0, head_size)], sems.at[3]),
    ]
    for copy in copies:
        copy.start()
    copies[0].wait()
    copies[1].wait()
    reflect = reflect_ref[...]
    reflect_float = reflect.astype(F32)
    square_high, square_low = halves(reflect_float * reflect_float)
    ones = jnp.ones((8, head_size), BF16)
    norms = dot_rows(ones, square_high) + dot_rows(ones, square_low)
    strength = 2.0 / (1.0 + jnp.exp(-logit_ref[...]))
    gains = strength / (norms + 1e-06)
    gain_ref[...] = gains
    gain = gains[0:1, :]
    rows = lax.broadcasted_iota(jnp.int32, (length, length), 0)
    columns = lax.broadcasted_iota(jnp.int32, (length, length), 1)
    strictly = rows > columns
    chained = jnp.where(strictly, dot_rows(reflect, reflect) * gain, 0.0)
    reflect_turned = reflect_float.T
    copies[2].wait()
    keys = keys_ref[...]
    facing = jnp.where(strictly, dot_rows(reflect, keys), 0.0)
    keys_turned = keys.astype(F32).T
    turned_ref[:, :length] = reflect_turned.astype(BF16)
    turned_ref[:, length:] = keys_turned.astype(BF16)
    scaled_high, scaled_low = halves(reflect_turned * gain)
    scaled_first = (scaled_high[:, :half], scaled_low[:, :half])
    scaled_second = (scaled_high[:, half:], scaled_low[:, half:])
    across = halves(chained[half:, :half])
    wide = halves(jnp.concatenate([facing[:half, :half], reflect_float[:half]], axis=1))
    tall = halves(
        jnp.concatenate([facing[half:, :half], reflect_float[half:], facing[half:, half:]], axis=1)
    )
    first, second = unit_inverses([chained[:half, :half], chained[half:, half:]])
    upper = dot_halves(halves(first), wide)
    reach = halves(dot_halves(scaled_second, halves(second)))
    bridge = dot_halves(reach, across)
    upper_halves = halves(upper)
    own = dot_halves(scaled_first, upper_halves)
    later = dot_halves(reach, tall)
    change = (own + later[:, :wide_size - half]) - dot_halves(halves(bridge), upper_halves)
    partial_ref[:, :half] = second
    partial_ref[:, half:length] = chained[half:, :half]
    partial_ref[:, length : 2 * length] = facing[half:, :]
    partial_ref[:, 2 * length :] = upper
    head_rows = lax.broadcasted_iota(jnp.int32, (head_size, head_size), 0)
    head_columns = lax.broadcasted_iota(jnp.int32, (head_size, head_size), 1)
    identity = (head_rows == head_columns).astype(F32)
    packet_ref[:, :half] = (keys_turned[:, :half] - change[:, :half]).astype(BF16)
    packet_ref[:, half:length] = (keys_turned[:, half:] - later[:, half + head_size :]).astype(BF16)
    packet_ref[:, length:wide_size] = (identity - change[:, half:]).astype(BF16)
    copies[3].wait()
    ones_ref[:, head_size:] = jnp.ones((length, head_size), BF16)
    for part in range(length // head_size):
        start = wide_size + part * head_size
        packet_ref[:, start : start + head_size] = ones_ref[
            part * head_size : (part + 1) * head_size, :head_size
        ]


def solve_rows(partial_ref, reflect_ref):
    length, head_size = reflect_ref.shape
    half = length // 2
    second = halves(partial_ref[:, :half])
    across = halves(partial_ref[:, half:length])
    facing = partial_ref[:, length : 2 * length]
    upper = partial_ref[:, 2 * length :]
    reflect = reflect_ref[half:, :].astype(F32)
    tall = jnp.concatenate([facing[:, :half], reflect, facing[:, half:]], axis=1)
    lower = dot_halves(second, halves(tall))
    bridge = dot_halves(second, across)
    lower_left = lower[:, : half + head_size] - dot_halves(halves(bridge), halves(upper))
    top = [upper[:, :half], jnp.zeros((half, half), F32), upper[:, half:]]
    bottom = [lower_left[:, :half], lower[:, half + head_size :], lower_left[:, half:]]
    return halves(
        jnp.concatenate([jnp.concatenate(top, axis=1), jnp.concatenate(bottom, axis=1)], axis=0)
    )


def lane_pieces(scores, size):
    return [score[:, i : i + size] for score in scores for i in range(0, score.shape[1], size)]


def row_peak(scores, peak):
    largest = functools.reduce(jnp.maximum, lane_pieces(scores, peak.shape[1]))
    return jnp.maximum(peak, jnp.max(largest, axis=1, keepdims=True))


def row_weights(scores, peak, rate):
    pieces = [jnp.exp2((piece - peak) * rate) for piece in lane_pieces(scores, peak.shape[1])]
    return jnp.concatenate(pieces, axis=1).astype(BF16)


def reciprocal(value):
    rough = pl.reciprocal(value, approx=True)
    return rough * (2.0 - value * rough)


def query_heads(heads, queries_ref, both_ref, ones_ref, solved, gain_ref, state_refs):
    turned_ref, peak_ref, total_ref, weighted_ref = state_refs
    length = ones_ref.shape[0]
    head_size = ones_ref.shape[1] // 2
    rate = math.log2(math.e) * head_size ** (-0.5)
    rows = lax.broadcasted_iota(jnp.int32, (length, length), 0)
    columns = lax.broadcasted_iota(jnp.int32, (length, length), 1)
    visible = rows >= columns
    gain = jnp.where(visible, gain_ref[0:1, :], 0.0)
    hidden = jnp.where(visible, 0.0, -1e30)
    both = both_ref[...]
    values = ones_ref[...]
    for head in heads:
        span = slice(head * head_size, (head + 1) * head_size)
        queries = queries_ref[:, span]
        faced = dot(queries, both)
        change = dot_halves(halves(faced[:, :length] * gain), solved)
        scores = (faced[:, length:] - change[:, :length]) + hidden
        turned_ref[:, span] = (queries.astype(F32) - change[:, length:]).astype(BF16)
        peak = jnp.broadcast_to(jnp.max(scores, axis=1, keepdims=True), (length, head_size))
        sums = dot(row_weights([scores], peak, rate), values)
        peak_ref[:, span] = peak
        weighted_ref[:, span] = sums[:, :head_size]
        total_ref[:, span] = sums[:, head_size:]


def first_queries(heads, longest, docs_hbm, *refs):
    queries_ref, both_ref, ones_ref, partial_ref, reflect_ref, gain_ref = refs[:6]
    state_refs = refs[6:10]
    present_ref, solved_ref, docs_ref, docs_sem = refs[10:]
    docs_copy = pltpu.make_async_copy(docs_hbm, docs_ref, docs_sem)
    docs_copy.start()
    solved = solve_rows(partial_ref, reflect_ref)
    wide_size = solved[0].shape[1]
    solved_ref[:, :wide_size] = solved[0]
    solved_ref[:, wide_size:] = solved[1]
    query_heads(heads, queries_ref, both_ref, ones_ref, solved, gain_ref, state_refs)
    docs_copy.wait()
    block = lax.axis_index("outer") * lax.axis_size("inner") + lax.axis_index("inner")
    own_doc = docs_ref[block]
    present = jnp.int32(0)
    for distance in range(1, longest):
        source = block - distance
        same = (source >= 0) & (docs_ref[jnp.maximum(source, 0)] == own_doc)
        present = present + same.astype(jnp.int32)
    state = 2 * present + block % 2
    present_ref[...] = jnp.full(present_ref.shape, state, jnp.int32)


def other_queries(heads, *refs):
    queries_ref, both_ref, ones_ref, solved_ref, gain_ref = refs[:5]
    state_refs = refs[9:]
    for done_ref, state_ref in zip(refs[5:9], state_refs):
        state_ref[:, : done_ref.shape[1]] = done_ref[...]
    wide_size = solved_ref.shape[1] // 2
    solved = (solved_ref[:, :wide_size], solved_ref[:, wide_size:])
    query_heads(heads, queries_ref, both_ref, ones_ref, solved, gain_ref, state_refs)


def present_and_odd(present_ref):
    state = present_ref[0, 0]
    return state // 2, state % 2 == 1


def put_out(out_ref, out_hbm, out_sems, head, head_size):
    span = slice(head * head_size, (head + 1) * head_size)
    return pltpu.make_async_copy(out_ref.at[:, span], out_hbm.at[:, span], out_sems.at[head])


def attend(head_count, state_refs, new_refs, all_keys, values, out_refs):
    turned_ref, peak_ref, total_ref, weighted_ref = state_refs
    head_size = turned_ref.shape[1] // head_count
    rate = math.log2(math.e) * head_size ** (-0.5)
    for head in range(head_count):
        span = slice(head * head_size, (head + 1) * head_size)
        old_peak = peak_ref[:, span]
        scores = [dot(turned_ref[:, span], keys) for keys in all_keys]
        peak = row_peak(scores, old_peak)
        sums = dot(row_weights(scores, peak, rate), values)
        factor = jnp.exp2((old_peak - peak) * rate)
        total = total_ref[:, span] * factor + sums[:, head_size:]
        weighted = weighted_ref[:, span] * factor + sums[:, :head_size]
        if out_refs is not None:
            out_refs[0][:, span] = (weighted * reciprocal(total)).astype(BF16)
            put_out(*out_refs, head, head_size).start()
        else:
            for new_ref, new in zip(new_refs, (peak, total, weighted)):
                new_ref[:, span] = new
    if out_refs is not None:
        wait_out(head_count, out_refs)


def finish(head_count, sum_refs, out_refs):
    total_ref, weighted_ref = sum_refs
    head_size = total_ref.shape[1] // head_count
    for head in range(head_count):
        span = slice(head * head_size, (head + 1) * head_size)
        out_refs[0][:, span] = (weighted_ref[:, span] * reciprocal(total_ref[:, span])).astype(BF16)
        put_out(*out_refs, head, head_size).start()
    wait_out(head_count, out_refs)


def wait_out(head_count, out_refs):
    head_size = out_refs[0].shape[1] // head_count
    for head in range(head_count):
        put_out(*out_refs, head, head_size).wait()


def store_values(values_ref, slot, place, packet, length):
    head_size = packet.shape[0]
    rows = pl.ds(place * length, length)
    start = length + head_size
    pieces = [
        packet[:, at : at + head_size] for at in range(start, start + length, head_size)
    ]
    values_ref[slot, rows, :head_size] = jnp.concatenate(pieces, axis=0)
    values_ref[slot, rows, head_size:] = jnp.ones((length, head_size), BF16)


def nearest(old_refs, new_refs, packet_ref, values_ref, out_refs):
    packet = packet_ref[...]
    length = values_ref.shape[1]
    head_count = old_refs[0].shape[1] // packet.shape[0]
    store_values(values_ref, 0, 0, packet, length)
    attend(head_count, old_refs, new_refs, [packet[:, :length]], values_ref[0], out_refs)


def nearest_kernel(head_count, present_ref, beside_ref, *refs):
    old_refs, new_refs = refs[:4], refs[4:7]
    out_hbm, out_ref, values_ref, out_sems = refs[7:]
    out_refs = (out_ref, out_hbm, out_sems)
    present, odd = present_and_odd(present_ref)

    @pl.when(present == 0)
    def _():
        finish(head_count, old_refs[2:], out_refs)

    @pl.when(odd & (present == 1))
    def _():
        nearest(old_refs, new_refs, beside_ref, values_ref, out_refs)

    @pl.when(odd & (present > 1))
    def _():
        nearest(old_refs, new_refs, beside_ref, values_ref, None)

    @pl.when(jnp.logical_not(odd) & (present > 0))
    def _():
        for old_ref, new_ref in zip(old_refs[1:], new_refs):
            new_ref[...] = old_ref[...]


def earlier_kernel(head_count, longest, present_ref, *refs):
    packet_refs = refs[:longest]
    state_refs = refs[longest : longest + 4]
    out_hbm, out_ref, keys_ref, values_ref, out_sems = refs[-5:]
    out_refs = (out_ref, out_hbm, out_sems)
    present, odd = present_and_odd(present_ref)
    length = out_ref.shape[0]
    head_size = out_ref.shape[1] // head_count
    wide_size = length + head_size
    steps = longest // 2 - 1
    apart_refs, swapped_refs = packet_refs[:steps], packet_refs[steps : 2 * steps]
    mixed_ref, beside_ref = packet_refs[2 * steps :]
    slots = values_ref.shape[0]

    def packet_of(distance, known_odd):
        if distance % 2 == 0:
            return apart_refs[distance // 2 - 1][...]
        odd_ref = beside_ref if distance == 1 else swapped_refs[(distance - 1) // 2 - 1]
        even_ref = mixed_ref if distance == longest - 1 else swapped_refs[(distance + 1) // 2 - 1]
        if known_odd is None:
            return jnp.where(odd, odd_ref[...], even_ref[...])
        return (odd_ref if known_odd else even_ref)[...]

    def collect(first, last, known_odd=None):
        transit = None
        all_keys = []
        for distance in range(1, last + 1):
            packet = packet_of(distance, known_odd)
            keys = packet[:, :length]
            own_transit = packet[:, length:wide_size]
            if distance == 1:
                transit = own_transit
            elif distance == 2:
                keys = dot(transit, keys).astype(BF16)
                if distance < last:
                    transit = dot(transit, own_transit)
            else:
                high, low = halves(transit)
                keys = (dot(high, keys) + dot(low, keys)).astype(BF16)
                if distance < last:
                    transit = dot(high, own_transit) + dot(low, own_transit)
            if distance >= first:
                all_keys.append(keys)
                index = distance - first
                store_values(values_ref, index // GROUP, index % GROUP, packet, length)
        return all_keys

    if slots == 1:
        for known_odd in (False, True):
            first = 2 if known_odd else 1
            for last in range(first, longest):

                @pl.when((odd == known_odd) & (present == last))
                def _(known_odd=known_odd, first=first, last=last):
                    keys = collect(first, last, known_odd)
                    values = values_ref[0, : len(keys) * length, :]
                    attend(head_count, state_refs, None, keys, values, out_refs)

    else:

        @pl.when(present > 0)
        def _():
            for index, keys in enumerate(collect(1, longest - 1)):
                slot, place = index // GROUP, index % GROUP
                keys_ref[slot, :, place * length : (place + 1) * length] = keys

        def visit(slot, blocks):
            keys = [keys_ref[slot, :, i * length : (i + 1) * length] for i in range(blocks)]
            values = values_ref[slot, : blocks * length, :]
            attend(head_count, state_refs, state_refs[1:], keys, values, None)

        full = present // GROUP

        @pl.loop(0, full)
        def _(slot):
            visit(slot, GROUP)

        for blocks in range(1, GROUP):
            pl.when(present % GROUP == blocks)(functools.partial(visit, full, blocks))
        finish(head_count, state_refs[2:], out_refs)


def vmem(count):
    return [pl.BlockSpec(memory_space=pltpu.VMEM)] * count


def in_hbm(value):
    return pltpu.with_memory_space_constraint(value, pltpu.HBM)


def permuted(value, target):
    count = lax.axis_size("outer") * lax.axis_size("inner")
    return lax.ppermute(value, AXES, [(i, target(i) % count) for i in range(count)])


def local(queries, keys, values, reflect, reflect_logit, doc_of_block):
    longest = lax.axis_size("outer") * lax.axis_size("inner") // 8
    length, head_size = keys.shape
    head_count = queries.shape[1] // head_size
    wide_size = length + head_size
    params = pltpu.CompilerParams(vmem_limit_bytes=VMEM_LIMIT)
    shape = jax.ShapeDtypeStruct
    hbm = pl.BlockSpec(memory_space=pltpu.HBM)
    packet, partial, gain, both, ones, reflect_rows = pl.pallas_call(
        key_kernel,
        out_shape=(
            shape((head_size, wide_size + length), BF16),
            shape((length // 2, 3 * length), F32),
            shape((8, length), F32),
            shape((head_size, 2 * length), BF16),
            shape((length, 2 * head_size), BF16),
            shape((length, head_size), BF16),
        ),
        in_specs=[hbm] * 4,
        out_specs=tuple(vmem(6)),
        scratch_shapes=[
            pltpu.VMEM((length, head_size), BF16),
            pltpu.VMEM((1, length), F32),
            pltpu.SemaphoreType.DMA((4,)),
        ],
        compiler_params=params,
        cost_estimate=pl.CostEstimate(
            flops=40 * length**3, bytes_accessed=8 * length * length, transcendentals=length
        ),
        name="key_side",
    )(*(in_hbm(value) for value in (reflect, keys, values, reflect_logit.reshape(1, length))))
    apart = [permuted(packet, lambda i, s=s: i + 2 * s) for s in range(1, longest // 2)]
    wide = shape(queries.shape, F32)
    state_shapes = (shape(queries.shape, BF16), wide, wide, wide)
    first = 1
    first_shapes = [shape((length, first * head_size), part.dtype) for part in state_shapes]

    def query_cost(heads):
        return pl.CostEstimate(
            flops=heads * 10 * length**3,
            bytes_accessed=16 * length * length * heads,
            transcendentals=heads * length * length,
        )

    *state, present, solved = pl.pallas_call(
        functools.partial(first_queries, range(first), longest),
        out_shape=(
            *first_shapes,
            shape((8, 128), jnp.int32),
            shape((length, 2 * wide_size), BF16),
        ),
        in_specs=[hbm] + vmem(6),
        out_specs=tuple(vmem(6)),
        scratch_shapes=[
            pltpu.SMEM(doc_of_block.shape, jnp.int32),
            pltpu.SemaphoreType.DMA(()),
        ],
        compiler_params=params,
        cost_estimate=query_cost(first),
        name="first_queries",
    )(in_hbm(doc_of_block), queries, both, ones, partial, reflect_rows, gain)
    mixed_packet, state[0] = lax.optimization_barrier((packet, state[0]))
    beside = permuted(mixed_packet, lambda i: i ^ 1)
    mixed = permuted(mixed_packet, lambda i: i + longest - 1 if i % 2 else i + 1)
    slots = (longest - 1 + GROUP - 1) // GROUP
    one_values = pltpu.VMEM((1, length, 2 * head_size), BF16)
    state = pl.pallas_call(
        functools.partial(other_queries, range(first, head_count)),
        out_shape=state_shapes,
        in_specs=vmem(9),
        out_specs=tuple(vmem(4)),
        compiler_params=params,
        cost_estimate=query_cost(head_count - first),
        name="other_queries",
    )(queries, both, ones, solved, gain, *state)
    *apart, turned = lax.optimization_barrier((*apart, state[0]))
    state = [turned, *state[1:]]
    swapped = [permuted(moved, lambda i: i ^ 1) for moved in apart]
    out_shape = shape(queries.shape, BF16)
    out_scratch = [pltpu.VMEM(queries.shape, BF16), pltpu.SemaphoreType.DMA((head_count,))]
    sums, started = state[1:], []
    if slots == 1:
        *sums, out = pl.pallas_call(
            functools.partial(nearest_kernel, head_count),
            out_shape=(*state_shapes[1:], out_shape),
            in_specs=vmem(6),
            out_specs=(*vmem(3), hbm),
            scratch_shapes=[
                out_scratch[0],
                one_values,
                out_scratch[1],
            ],
            compiler_params=params,
            cost_estimate=pl.CostEstimate(
                flops=head_count * 2 * length**3,
                bytes_accessed=4 * length * length * head_count,
                transcendentals=head_count * length * length,
            ),
            name="nearest_block",
        )(present, beside, *state)
        started = [in_hbm(out)]
    return pl.pallas_call(
        functools.partial(earlier_kernel, head_count, longest),
        out_shape=out_shape,
        in_specs=vmem(longest + 5) + [hbm] * len(started),
        out_specs=hbm,
        input_output_aliases={longest + 5: 0} if started else {},
        scratch_shapes=[
            out_scratch[0],
            pltpu.VMEM((slots, head_size, GROUP * length), BF16),
            pltpu.VMEM((slots, GROUP * length, 2 * head_size), BF16),
            out_scratch[1],
        ],
        compiler_params=params,
        cost_estimate=pl.CostEstimate(
            flops=head_count * 6 * length**3,
            bytes_accessed=16 * length * length * head_count,
            transcendentals=3 * head_count * length * length,
        ),
        name="earlier_blocks",
    )(present, *apart, *swapped, mixed, beside, turned, *sums, *started)


def solution(mesh):
    placed = (
        P(AXES, None),
        P(AXES, None),
        P(AXES, None),
        P(AXES, None),
        P(AXES),
        P(),
    )
    return jax.shard_map(
        local, mesh=mesh, in_specs=placed, out_specs=P(AXES, None), check_vma=False
    )
```

```python
import functools
import math

import jax
import jax.numpy as jnp
from jax import lax
from jax.experimental import pallas as pl
from jax.experimental.pallas import tpu as pltpu
from jax.sharding import PartitionSpec as P

F32 = jnp.float32
BF16 = jnp.bfloat16
AXES = ("outer", "inner")
GROUP = 3
VMEM_LIMIT = 24 * 1024 * 1024


def dot(left, right):
    return jnp.dot(left, right, preferred_element_type=F32)


def dot_rows(left, right):
    return lax.dot_general(left, right, (((1,), (1,)), ((), ())), preferred_element_type=F32)


def halves(value):
    high = value.astype(BF16)
    return high, (value - high.astype(F32)).astype(BF16)


def dot_halves(left, right):
    (left_high, left_low), (right_high, right_low) = left, right
    return dot(left_high, right_high) + (dot(left_high, right_low) + dot(left_low, right_high))


def unit_inverses(strict_parts):
    length = strict_parts[0].shape[0]
    rows = lax.broadcasted_iota(jnp.int32, (length, length), 0)
    columns = lax.broadcasted_iota(jnp.int32, (length, length), 1)
    identity = (rows == columns).astype(F32)
    results = [identity - part for part in strict_parts]
    powers = [halves(part) for part in strict_parts]
    powers = [dot_halves(power, power) for power in powers]
    reach = 4
    while reach < length:
        for index, (result, power) in enumerate(zip(results, powers)):
            high, low = halves(jnp.concatenate([power, result], axis=0))
            weights = (high[:length], low[:length])
            product = dot_halves((high, low), weights)
            powers[index] = product[:length]
            results[index] = result + product[length:]
        reach = reach * 2
    return [
        result + dot_halves(halves(result), halves(power))
        for result, power in zip(results, powers)
    ]


def key_kernel(
    reflect_hbm,
    keys_hbm,
    values_hbm,
    logit_hbm,
    packet_ref,
    partial_ref,
    gain_ref,
    turned_ref,
    ones_ref,
    reflect_ref,
    keys_ref,
    logit_ref,
    sems,
):
    length, head_size = reflect_ref.shape
    half = length // 2
    wide_size = length + head_size
    copies = [
        pltpu.make_async_copy(reflect_hbm, reflect_ref, sems.at[0]),
        pltpu.make_async_copy(logit_hbm, logit_ref, sems.at[1]),
        pltpu.make_async_copy(keys_hbm, keys_ref, sems.at[2]),
        pltpu.make_async_copy(values_hbm, ones_ref.at[:, pl.ds(0, head_size)], sems.at[3]),
    ]
    for copy in copies:
        copy.start()
    copies[0].wait()
    copies[1].wait()
    reflect = reflect_ref[...]
    reflect_float = reflect.astype(F32)
    square_high, square_low = halves(reflect_float * reflect_float)
    ones = jnp.ones((8, head_size), BF16)
    norms = dot_rows(ones, square_high) + dot_rows(ones, square_low)
    strength = 2.0 / (1.0 + jnp.exp(-logit_ref[...]))
    gains = strength / (norms + 1e-06)
    gain_ref[...] = gains
    gain = gains[0:1, :]
    rows = lax.broadcasted_iota(jnp.int32, (length, length), 0)
    columns = lax.broadcasted_iota(jnp.int32, (length, length), 1)
    strictly = rows > columns
    chained = jnp.where(strictly, dot_rows(reflect, reflect) * gain, 0.0)
    reflect_turned = reflect_float.T
    copies[2].wait()
    keys = keys_ref[...]
    facing = jnp.where(strictly, dot_rows(reflect, keys), 0.0)
    keys_turned = keys.astype(F32).T
    turned_ref[:, :length] = reflect_turned.astype(BF16)
    turned_ref[:, length:] = keys_turned.astype(BF16)
    scaled_high, scaled_low = halves(reflect_turned * gain)
    scaled_first = (scaled_high[:, :half], scaled_low[:, :half])
    scaled_second = (scaled_high[:, half:], scaled_low[:, half:])
    across = halves(chained[half:, :half])
    wide = halves(jnp.concatenate([facing[:half, :half], reflect_float[:half]], axis=1))
    tall = halves(
        jnp.concatenate([facing[half:, :half], reflect_float[half:], facing[half:, half:]], axis=1)
    )
    first, second = unit_inverses([chained[:half, :half], chained[half:, half:]])
    upper = dot_halves(halves(first), wide)
    reach = halves(dot_halves(scaled_second, halves(second)))
    bridge = dot_halves(reach, across)
    upper_halves = halves(upper)
    own = dot_halves(scaled_first, upper_halves)
    later = dot_halves(reach, tall)
    change = (own + later[:, :wide_size - half]) - dot_halves(halves(bridge), upper_halves)
    partial_ref[:, :half] = second
    partial_ref[:, half:length] = chained[half:, :half]
    partial_ref[:, length : 2 * length] = facing[half:, :]
    partial_ref[:, 2 * length :] = upper
    head_rows = lax.broadcasted_iota(jnp.int32, (head_size, head_size), 0)
    head_columns = lax.broadcasted_iota(jnp.int32, (head_size, head_size), 1)
    identity = (head_rows == head_columns).astype(F32)
    packet_ref[:, :half] = (keys_turned[:, :half] - change[:, :half]).astype(BF16)
    packet_ref[:, half:length] = (keys_turned[:, half:] - later[:, half + head_size :]).astype(BF16)
    packet_ref[:, length:wide_size] = (identity - change[:, half:]).astype(BF16)
    copies[3].wait()
    ones_ref[:, head_size:] = jnp.ones((length, head_size), BF16)
    for part in range(length // head_size):
        start = wide_size + part * head_size
        packet_ref[:, start : start + head_size] = ones_ref[
            part * head_size : (part + 1) * head_size, :head_size
        ]


def solve_rows(partial_ref, reflect_ref):
    length, head_size = reflect_ref.shape
    half = length // 2
    second = halves(partial_ref[:, :half])
    across = halves(partial_ref[:, half:length])
    facing = partial_ref[:, length : 2 * length]
    upper = partial_ref[:, 2 * length :]
    reflect = reflect_ref[half:, :].astype(F32)
    tall = jnp.concatenate([facing[:, :half], reflect, facing[:, half:]], axis=1)
    lower = dot_halves(second, halves(tall))
    bridge = dot_halves(second, across)
    lower_left = lower[:, : half + head_size] - dot_halves(halves(bridge), halves(upper))
    top = [upper[:, :half], jnp.zeros((half, half), F32), upper[:, half:]]
    bottom = [lower_left[:, :half], lower[:, half + head_size :], lower_left[:, half:]]
    return halves(
        jnp.concatenate([jnp.concatenate(top, axis=1), jnp.concatenate(bottom, axis=1)], axis=0)
    )


def lane_pieces(scores, size):
    return [score[:, i : i + size] for score in scores for i in range(0, score.shape[1], size)]


def row_peak(scores, peak):
    largest = functools.reduce(jnp.maximum, lane_pieces(scores, peak.shape[1]))
    return jnp.maximum(peak, jnp.max(largest, axis=1, keepdims=True))


def row_weights(scores, peak, rate):
    pieces = [jnp.exp2((piece - peak) * rate) for piece in lane_pieces(scores, peak.shape[1])]
    return jnp.concatenate(pieces, axis=1).astype(BF16)


def reciprocal(value):
    rough = pl.reciprocal(value, approx=True)
    return rough * (2.0 - value * rough)


def query_heads(heads, queries_ref, both_ref, ones_ref, solved, gain_ref, state_refs):
    turned_ref, peak_ref, total_ref, weighted_ref = state_refs
    length = ones_ref.shape[0]
    head_size = ones_ref.shape[1] // 2
    rate = math.log2(math.e) * head_size ** (-0.5)
    rows = lax.broadcasted_iota(jnp.int32, (length, length), 0)
    columns = lax.broadcasted_iota(jnp.int32, (length, length), 1)
    visible = rows >= columns
    gain = jnp.where(visible, gain_ref[0:1, :], 0.0)
    hidden = jnp.where(visible, 0.0, -1e30)
    both = both_ref[...]
    values = ones_ref[...]
    for head in heads:
        span = slice(head * head_size, (head + 1) * head_size)
        queries = queries_ref[:, span]
        faced = dot(queries, both)
        change = dot_halves(halves(faced[:, :length] * gain), solved)
        scores = (faced[:, length:] - change[:, :length]) + hidden
        turned_ref[:, span] = (queries.astype(F32) - change[:, length:]).astype(BF16)
        peak = jnp.broadcast_to(jnp.max(scores, axis=1, keepdims=True), (length, head_size))
        sums = dot(row_weights([scores], peak, rate), values)
        peak_ref[:, span] = peak
        weighted_ref[:, span] = sums[:, :head_size]
        total_ref[:, span] = sums[:, head_size:]


def first_queries(heads, *refs):
    queries_ref, both_ref, ones_ref, partial_ref, reflect_ref, gain_ref = refs[:6]
    *state_refs, solved_ref = refs[6:]
    solved = solve_rows(partial_ref, reflect_ref)
    wide_size = solved[0].shape[1]
    solved_ref[:, :wide_size] = solved[0]
    solved_ref[:, wide_size:] = solved[1]
    query_heads(heads, queries_ref, both_ref, ones_ref, solved, gain_ref, state_refs)


def other_queries(heads, longest, docs_hbm, *refs):
    queries_ref, both_ref, ones_ref, solved_ref, gain_ref = refs[:5]
    *state_refs, present_ref, docs_ref, docs_sem = refs[9:]
    docs_copy = pltpu.make_async_copy(docs_hbm, docs_ref, docs_sem)
    docs_copy.start()
    for done_ref, state_ref in zip(refs[5:9], state_refs):
        state_ref[:, : done_ref.shape[1]] = done_ref[...]
    wide_size = solved_ref.shape[1] // 2
    solved = (solved_ref[:, :wide_size], solved_ref[:, wide_size:])
    query_heads(heads, queries_ref, both_ref, ones_ref, solved, gain_ref, state_refs)
    docs_copy.wait()
    block = lax.axis_index("outer") * lax.axis_size("inner") + lax.axis_index("inner")
    own_doc = docs_ref[block]
    present = jnp.int32(0)
    for distance in range(1, longest):
        source = block - distance
        same = (source >= 0) & (docs_ref[jnp.maximum(source, 0)] == own_doc)
        present = present + same.astype(jnp.int32)
    state = 2 * present + block % 2
    present_ref[...] = jnp.full(present_ref.shape, state, jnp.int32)


def present_and_odd(present_ref):
    state = present_ref[0, 0]
    return state // 2, state % 2 == 1


def put_out(out_ref, out_hbm, out_sems, head, head_size):
    span = slice(head * head_size, (head + 1) * head_size)
    return pltpu.make_async_copy(out_ref.at[:, span], out_hbm.at[:, span], out_sems.at[head])


def attend(heads, state_refs, new_refs, all_keys, values, out_refs):
    turned_ref, peak_ref, total_ref, weighted_ref = state_refs
    head_size = values.shape[1] // 2
    rate = math.log2(math.e) * head_size ** (-0.5)
    for head in heads:
        span = slice(head * head_size, (head + 1) * head_size)
        old_peak = peak_ref[:, span]
        scores = [dot(turned_ref[:, span], keys) for keys in all_keys]
        peak = row_peak(scores, old_peak)
        sums = dot(row_weights(scores, peak, rate), values)
        factor = jnp.exp2((old_peak - peak) * rate)
        total = total_ref[:, span] * factor + sums[:, head_size:]
        weighted = weighted_ref[:, span] * factor + sums[:, :head_size]
        if out_refs is not None:
            out_refs[0][:, span] = (weighted * reciprocal(total)).astype(BF16)
            if len(out_refs) > 1:
                put_out(*out_refs, head, head_size).start()
        else:
            for new_ref, new in zip(new_refs, (peak, total, weighted)):
                new_ref[:, span] = new
    if out_refs is not None and len(out_refs) > 1:
        wait_out(heads, out_refs, head_size)


def finish(head_count, sum_refs, out_refs):
    total_ref, weighted_ref = sum_refs
    head_size = total_ref.shape[1] // head_count
    for head in range(head_count):
        span = slice(head * head_size, (head + 1) * head_size)
        out_refs[0][:, span] = (weighted_ref[:, span] * reciprocal(total_ref[:, span])).astype(BF16)
        put_out(*out_refs, head, head_size).start()
    wait_out(range(head_count), out_refs, head_size)


def wait_out(heads, out_refs, head_size):
    for head in heads:
        put_out(*out_refs, head, head_size).wait()


def store_values(values_ref, slot, place, packet, length):
    head_size = packet.shape[0]
    rows = pl.ds(place * length, length)
    start = length + head_size
    pieces = [
        packet[:, at : at + head_size] for at in range(start, start + length, head_size)
    ]
    values_ref[slot, rows, :head_size] = jnp.concatenate(pieces, axis=0)
    values_ref[slot, rows, head_size:] = jnp.ones((length, head_size), BF16)


def nearest(heads, old_refs, new_refs, packet_ref, values_ref, out_refs):
    packet = packet_ref[...]
    length = values_ref.shape[1]
    store_values(values_ref, 0, 0, packet, length)
    attend(heads, old_refs, new_refs, [packet[:, :length]], values_ref[0], out_refs)


def is_first_odd():
    return (lax.axis_index("outer") == 0) & (lax.axis_index("inner") == 1)


def early_kernel(heads, present_ref, beside_ref, *refs):
    *state_refs, done_ref, values_ref = refs
    present, _ = present_and_odd(present_ref)

    @pl.when(is_first_odd() & (present == 1))
    def _():
        nearest(heads, state_refs, None, beside_ref, values_ref, (done_ref,))


def nearest_kernel(head_count, early_heads, present_ref, beside_ref, done_ref, *refs):
    old_refs, new_refs = refs[:4], refs[4:7]
    out_hbm, out_ref, values_ref, out_sems = refs[7:]
    out_refs = (out_ref, out_hbm, out_sems)
    present, odd = present_and_odd(present_ref)
    first_odd = is_first_odd()
    heads = range(head_count)

    @pl.when(present == 0)
    def _():
        finish(head_count, old_refs[2:], out_refs)

    @pl.when(first_odd & (present == 1))
    def _():
        head_size = beside_ref.shape[0]
        done_refs = (done_ref, out_hbm, out_sems)
        for head in heads[:early_heads]:
            put_out(*done_refs, head, head_size).start()
        if early_heads < head_count:
            nearest(heads[early_heads:], old_refs, new_refs, beside_ref, values_ref, out_refs)
        wait_out(heads[:early_heads], done_refs, head_size)

    @pl.when(odd & (present == 1) & jnp.logical_not(first_odd))
    def _():
        nearest(heads, old_refs, new_refs, beside_ref, values_ref, out_refs)

    @pl.when(odd & (present > 1))
    def _():
        nearest(heads, old_refs, new_refs, beside_ref, values_ref, None)

    @pl.when(jnp.logical_not(odd) & (present > 0))
    def _():
        for old_ref, new_ref in zip(old_refs[1:], new_refs):
            new_ref[...] = old_ref[...]


def earlier_kernel(head_count, longest, present_ref, *refs):
    packet_refs = refs[:longest]
    state_refs = refs[longest : longest + 4]
    out_hbm, out_ref, keys_ref, values_ref, out_sems = refs[-5:]
    out_refs = (out_ref, out_hbm, out_sems)
    present, odd = present_and_odd(present_ref)
    length = out_ref.shape[0]
    head_size = out_ref.shape[1] // head_count
    wide_size = length + head_size
    steps = longest // 2 - 1
    apart_refs, swapped_refs = packet_refs[:steps], packet_refs[steps : 2 * steps]
    mixed_ref, beside_ref = packet_refs[2 * steps :]
    slots = values_ref.shape[0]

    def packet_of(distance, known_odd):
        if distance % 2 == 0:
            return apart_refs[distance // 2 - 1][...]
        odd_ref = beside_ref if distance == 1 else swapped_refs[(distance - 1) // 2 - 1]
        even_ref = mixed_ref if distance == longest - 1 else swapped_refs[(distance + 1) // 2 - 1]
        if known_odd is None:
            return jnp.where(odd, odd_ref[...], even_ref[...])
        return (odd_ref if known_odd else even_ref)[...]

    def collect(first, last, known_odd=None):
        transit = None
        all_keys = []
        for distance in range(1, last + 1):
            packet = packet_of(distance, known_odd)
            keys = packet[:, :length]
            own_transit = packet[:, length:wide_size]
            if distance == 1:
                transit = own_transit
            elif distance == 2:
                keys = dot(transit, keys).astype(BF16)
                if distance < last:
                    transit = dot(transit, own_transit)
            else:
                high, low = halves(transit)
                keys = (dot(high, keys) + dot(low, keys)).astype(BF16)
                if distance < last:
                    transit = dot(high, own_transit) + dot(low, own_transit)
            if distance >= first:
                all_keys.append(keys)
                index = distance - first
                store_values(values_ref, index // GROUP, index % GROUP, packet, length)
        return all_keys

    def take(first, last, known_odd):
        keys = collect(first, last, known_odd)
        values = values_ref[0, : len(keys) * length, :]
        attend(range(head_count), state_refs, None, keys, values, out_refs)

    def choose(first, last, known_odd):
        if first == last:
            take(2 if known_odd else 1, last, known_odd)
        else:
            middle = (first + last + 1) // 2
            lax.cond(
                present >= middle,
                lambda: choose(middle, last, known_odd),
                lambda: choose(first, middle - 1, known_odd),
            )

    if slots == 1:

        @pl.when(present > odd.astype(jnp.int32))
        def _():
            lax.cond(
                odd,
                lambda: choose(2, longest - 1, True),
                lambda: choose(1, longest - 1, False),
            )

    else:

        @pl.when(present > 0)
        def _():
            for index, keys in enumerate(collect(1, longest - 1)):
                slot, place = index // GROUP, index % GROUP
                keys_ref[slot, :, place * length : (place + 1) * length] = keys

        def visit(slot, blocks):
            keys = [keys_ref[slot, :, i * length : (i + 1) * length] for i in range(blocks)]
            values = values_ref[slot, : blocks * length, :]
            attend(range(head_count), state_refs, state_refs[1:], keys, values, None)

        full = present // GROUP

        @pl.loop(0, full)
        def _(slot):
            visit(slot, GROUP)

        for blocks in range(1, GROUP):
            pl.when(present % GROUP == blocks)(functools.partial(visit, full, blocks))
        finish(head_count, state_refs[2:], out_refs)


def vmem(count):
    return [pl.BlockSpec(memory_space=pltpu.VMEM)] * count


def in_hbm(value):
    return pltpu.with_memory_space_constraint(value, pltpu.HBM)


def permuted(value, target):
    count = lax.axis_size("outer") * lax.axis_size("inner")
    return lax.ppermute(value, AXES, [(i, target(i) % count) for i in range(count)])


def local(queries, keys, values, reflect, reflect_logit, doc_of_block):
    longest = lax.axis_size("outer") * lax.axis_size("inner") // 8
    length, head_size = keys.shape
    head_count = queries.shape[1] // head_size
    wide_size = length + head_size
    params = pltpu.CompilerParams(vmem_limit_bytes=VMEM_LIMIT)
    shape = jax.ShapeDtypeStruct
    hbm = pl.BlockSpec(memory_space=pltpu.HBM)
    packet, partial, gain, both, ones, reflect_rows = pl.pallas_call(
        key_kernel,
        out_shape=(
            shape((head_size, wide_size + length), BF16),
            shape((length // 2, 3 * length), F32),
            shape((8, length), F32),
            shape((head_size, 2 * length), BF16),
            shape((length, 2 * head_size), BF16),
            shape((length, head_size), BF16),
        ),
        in_specs=[hbm] * 4,
        out_specs=tuple(vmem(6)),
        scratch_shapes=[
            pltpu.VMEM((length, head_size), BF16),
            pltpu.VMEM((1, length), F32),
            pltpu.SemaphoreType.DMA((4,)),
        ],
        compiler_params=params,
        cost_estimate=pl.CostEstimate(
            flops=40 * length**3, bytes_accessed=8 * length * length, transcendentals=length
        ),
        name="key_side",
    )(*(in_hbm(value) for value in (reflect, keys, values, reflect_logit.reshape(1, length))))
    apart = [permuted(packet, lambda i, s=s: i + 2 * s) for s in range(1, longest // 2)]
    wide = shape(queries.shape, F32)
    state_shapes = (shape(queries.shape, BF16), wide, wide, wide)
    first = max(1, head_count // 4)
    first_shapes = [shape((length, first * head_size), part.dtype) for part in state_shapes]

    def query_cost(heads):
        return pl.CostEstimate(
            flops=heads * 10 * length**3,
            bytes_accessed=16 * length * length * heads,
            transcendentals=heads * length * length,
        )

    *state, solved = pl.pallas_call(
        functools.partial(first_queries, range(first)),
        out_shape=(*first_shapes, shape((length, 2 * wide_size), BF16)),
        in_specs=vmem(6),
        out_specs=tuple(vmem(5)),
        compiler_params=params,
        cost_estimate=query_cost(first),
        name="first_queries",
    )(queries, both, ones, partial, reflect_rows, gain)
    mixed_packet, state[0] = lax.optimization_barrier((packet, state[0]))
    beside = permuted(mixed_packet, lambda i: i ^ 1)
    mixed = permuted(mixed_packet, lambda i: i + longest - 1 if i % 2 else i + 1)
    slots = (longest - 1 + GROUP - 1) // GROUP
    one_values = pltpu.VMEM((1, length, 2 * head_size), BF16)
    *state, present = pl.pallas_call(
        functools.partial(other_queries, range(first, head_count), longest),
        out_shape=(*state_shapes, shape((8, 128), jnp.int32)),
        in_specs=[hbm] + vmem(9),
        out_specs=tuple(vmem(5)),
        scratch_shapes=[
            pltpu.SMEM(doc_of_block.shape, jnp.int32),
            pltpu.SemaphoreType.DMA(()),
        ],
        compiler_params=params,
        cost_estimate=query_cost(head_count - first),
        name="other_queries",
    )(in_hbm(doc_of_block), queries, both, ones, solved, gain, *state)
    out_shape = shape(queries.shape, BF16)
    slots = (longest - 1 + GROUP - 1) // GROUP
    one_values = pltpu.VMEM((1, length, 2 * head_size), BF16)
    out_scratch = [pltpu.VMEM(queries.shape, BF16), pltpu.SemaphoreType.DMA((head_count,))]
    nearest_cost = pl.CostEstimate(
        flops=head_count * 2 * length**3,
        bytes_accessed=4 * length * length * head_count,
        transcendentals=head_count * length * length,
    )
    turned = state[0]
    *apart, present = lax.optimization_barrier((*apart, present))
    early_heads = head_count
    if slots == 1:
        done = pl.pallas_call(
            functools.partial(early_kernel, range(early_heads)),
            out_shape=shape((length, early_heads * head_size), BF16),
            in_specs=vmem(6),
            out_specs=vmem(1)[0],
            scratch_shapes=[one_values],
            compiler_params=params,
            cost_estimate=pl.CostEstimate(flops=0, bytes_accessed=0, transcendentals=0),
            name="early_heads",
        )(present, beside, *state)
        *apart, done = lax.optimization_barrier((*apart, done))
    swapped = [permuted(moved, lambda i: i ^ 1) for moved in apart]
    sums, started = state[1:], []
    if slots == 1:
        *sums, out = pl.pallas_call(
            functools.partial(nearest_kernel, head_count, early_heads),
            out_shape=(*state_shapes[1:], out_shape),
            in_specs=vmem(7),
            out_specs=(*vmem(3), hbm),
            scratch_shapes=[out_scratch[0], one_values, out_scratch[1]],
            compiler_params=params,
            cost_estimate=nearest_cost,
            name="nearest_block",
        )(present, beside, done, *state)
        started = [in_hbm(out)]
    return pl.pallas_call(
        functools.partial(earlier_kernel, head_count, longest),
        out_shape=out_shape,
        in_specs=vmem(longest + 5) + [hbm] * len(started),
        out_specs=hbm,
        input_output_aliases={longest + 5: 0} if started else {},
        scratch_shapes=[
            out_scratch[0],
            pltpu.VMEM((slots, head_size, GROUP * length), BF16),
            pltpu.VMEM((slots, GROUP * length, 2 * head_size), BF16),
            out_scratch[1],
        ],
        compiler_params=params,
        cost_estimate=pl.CostEstimate(
            flops=head_count * 6 * length**3,
            bytes_accessed=16 * length * length * head_count,
            transcendentals=3 * head_count * length * length,
        ),
        name="earlier_blocks",
    )(present, *apart, *swapped, mixed, beside, turned, *sums, *started)


def solution(mesh):
    placed = (
        P(AXES, None),
        P(AXES, None),
        P(AXES, None),
        P(AXES, None),
        P(AXES),
        P(),
    )
    return jax.shard_map(
        local, mesh=mesh, in_specs=placed, out_specs=P(AXES, None), check_vma=False
    )
```

```python
import functools
import math

import jax
import jax.numpy as jnp
from jax import lax
from jax.experimental import pallas as pl
from jax.experimental.pallas import tpu as pltpu
from jax.sharding import PartitionSpec as P

F32 = jnp.float32
BF16 = jnp.bfloat16
AXES = ("outer", "inner")
GROUP = 3
VMEM_LIMIT = 24 * 1024 * 1024


def dot(left, right):
    return jnp.dot(left, right, preferred_element_type=F32)


def dot_rows(left, right):
    return lax.dot_general(left, right, (((1,), (1,)), ((), ())), preferred_element_type=F32)


def halves(value):
    high = value.astype(BF16)
    return high, (value - high.astype(F32)).astype(BF16)


def dot_halves(left, right):
    (left_high, left_low), (right_high, right_low) = left, right
    return dot(left_high, right_high) + (dot(left_high, right_low) + dot(left_low, right_high))


def dot_joined(left, right):
    (left_high, left_low), (right_high, right_low) = left, right
    return dot(
        jnp.concatenate([left_high, left_low, left_high], axis=1),
        jnp.concatenate([right_high, right_high, right_low], axis=0),
    )


def unit_inverses(strict_parts):
    length = strict_parts[0].shape[0]
    rows = lax.broadcasted_iota(jnp.int32, (length, length), 0)
    columns = lax.broadcasted_iota(jnp.int32, (length, length), 1)
    identity = (rows == columns).astype(F32)
    results = [identity - part for part in strict_parts]
    powers = list(strict_parts)
    reach = 2
    while reach < length:
        for index, (result, power) in enumerate(zip(results, powers)):
            power = halves(power)
            powers[index] = dot_joined(power, power)
            if reach > 2:
                results[index] = result + dot_joined(halves(result), power)
        reach = reach * 2
    return [
        result + dot_joined(halves(result), halves(power))
        for result, power in zip(results, powers)
    ]


def key_kernel(
    reflect_hbm,
    keys_hbm,
    values_hbm,
    logit_hbm,
    packet_ref,
    partial_ref,
    gain_ref,
    turned_ref,
    ones_ref,
    reflect_ref,
    keys_ref,
    logit_ref,
    sems,
):
    length, head_size = reflect_ref.shape
    half = length // 2
    wide_size = length + head_size
    copies = [
        pltpu.make_async_copy(reflect_hbm, reflect_ref, sems.at[0]),
        pltpu.make_async_copy(logit_hbm, logit_ref, sems.at[1]),
        pltpu.make_async_copy(keys_hbm, keys_ref, sems.at[2]),
        pltpu.make_async_copy(values_hbm, ones_ref.at[:, pl.ds(0, head_size)], sems.at[3]),
    ]
    for copy in copies:
        copy.start()
    copies[0].wait()
    copies[1].wait()
    reflect = reflect_ref[...]
    reflect_float = reflect.astype(F32)
    square_high, square_low = halves(reflect_float * reflect_float)
    ones = jnp.ones((8, head_size), BF16)
    norms = dot_rows(ones, square_high) + dot_rows(ones, square_low)
    strength = 2.0 / (1.0 + jnp.exp(-logit_ref[...]))
    gains = strength / (norms + 1e-06)
    gain_ref[...] = gains
    gain = gains[0:1, :]
    rows = lax.broadcasted_iota(jnp.int32, (length, length), 0)
    columns = lax.broadcasted_iota(jnp.int32, (length, length), 1)
    strictly = rows > columns
    chained = jnp.where(strictly, dot_rows(reflect, reflect) * gain, 0.0)
    reflect_turned = reflect_float.T
    copies[2].wait()
    keys = keys_ref[...]
    facing = jnp.where(strictly, dot_rows(reflect, keys), 0.0)
    keys_turned = keys.astype(F32).T
    turned_ref[:, :length] = reflect_turned.astype(BF16)
    turned_ref[:, length:] = keys_turned.astype(BF16)
    scaled_high, scaled_low = halves(reflect_turned * gain)
    scaled_first = (scaled_high[:, :half], scaled_low[:, :half])
    scaled_second = (scaled_high[:, half:], scaled_low[:, half:])
    across = halves(chained[half:, :half])
    wide = halves(jnp.concatenate([facing[:half, :half], reflect_float[:half]], axis=1))
    tall = halves(
        jnp.concatenate([facing[half:, :half], reflect_float[half:], facing[half:, half:]], axis=1)
    )
    first, second = unit_inverses([chained[:half, :half], chained[half:, half:]])
    upper = dot_joined(halves(first), wide)
    reach = halves(dot_joined(scaled_second, halves(second)))
    bridge = dot_joined(reach, across)
    upper_halves = halves(upper)
    own = dot_joined(scaled_first, upper_halves)
    later = dot_joined(reach, tall)
    change = (own + later[:, :wide_size - half]) - dot_joined(halves(bridge), upper_halves)
    partial_ref[:, :half] = second
    partial_ref[:, half:length] = chained[half:, :half]
    partial_ref[:, length : 2 * length] = facing[half:, :]
    partial_ref[:, 2 * length :] = upper
    head_rows = lax.broadcasted_iota(jnp.int32, (head_size, head_size), 0)
    head_columns = lax.broadcasted_iota(jnp.int32, (head_size, head_size), 1)
    identity = (head_rows == head_columns).astype(F32)
    packet_ref[:, :half] = (keys_turned[:, :half] - change[:, :half]).astype(BF16)
    packet_ref[:, half:length] = (keys_turned[:, half:] - later[:, half + head_size :]).astype(BF16)
    packet_ref[:, length:wide_size] = (identity - change[:, half:]).astype(BF16)
    copies[3].wait()
    ones_ref[:, head_size:] = jnp.ones((length, head_size), BF16)
    for part in range(length // head_size):
        start = wide_size + part * head_size
        packet_ref[:, start : start + head_size] = ones_ref[
            part * head_size : (part + 1) * head_size, :head_size
        ]


def solve_rows(partial_ref, reflect_ref):
    length, head_size = reflect_ref.shape
    half = length // 2
    second = halves(partial_ref[:, :half])
    across = halves(partial_ref[:, half:length])
    facing = partial_ref[:, length : 2 * length]
    upper = partial_ref[:, 2 * length :]
    reflect = reflect_ref[half:, :].astype(F32)
    tall = jnp.concatenate([facing[:, :half], reflect, facing[:, half:]], axis=1)
    lower = dot_halves(second, halves(tall))
    bridge = dot_halves(second, across)
    lower_left = lower[:, : half + head_size] - dot_halves(halves(bridge), halves(upper))
    top = [upper[:, :half], jnp.zeros((half, half), F32), upper[:, half:]]
    bottom = [lower_left[:, :half], lower[:, half + head_size :], lower_left[:, half:]]
    return halves(
        jnp.concatenate([jnp.concatenate(top, axis=1), jnp.concatenate(bottom, axis=1)], axis=0)
    )


def lane_pieces(scores, size):
    return [score[:, i : i + size] for score in scores for i in range(0, score.shape[1], size)]


def row_peak(scores, peak):
    largest = functools.reduce(jnp.maximum, lane_pieces(scores, peak.shape[1]))
    return jnp.maximum(peak, jnp.max(largest, axis=1, keepdims=True))


def row_weights(scores, peak, rate):
    pieces = [jnp.exp2((piece - peak) * rate) for piece in lane_pieces(scores, peak.shape[1])]
    return jnp.concatenate(pieces, axis=1).astype(BF16)


def reciprocal(value):
    rough = pl.reciprocal(value, approx=True)
    return rough * (2.0 - value * rough)


def query_heads(heads, queries_ref, both_ref, ones_ref, solved, gain_ref, state_refs):
    turned_ref, peak_ref, total_ref, weighted_ref = state_refs
    length = ones_ref.shape[0]
    head_size = ones_ref.shape[1] // 2
    rate = math.log2(math.e) * head_size ** (-0.5)
    rows = lax.broadcasted_iota(jnp.int32, (length, length), 0)
    columns = lax.broadcasted_iota(jnp.int32, (length, length), 1)
    visible = rows >= columns
    gain = jnp.where(visible, gain_ref[0:1, :], 0.0)
    hidden = jnp.where(visible, 0.0, -1e30)
    both = both_ref[...]
    values = ones_ref[...]
    for head in heads:
        span = slice(head * head_size, (head + 1) * head_size)
        queries = queries_ref[:, span]
        faced = dot(queries, both)
        change = dot_halves(halves(faced[:, :length] * gain), solved)
        scores = (faced[:, length:] - change[:, :length]) + hidden
        turned_ref[:, span] = (queries.astype(F32) - change[:, length:]).astype(BF16)
        peak = jnp.broadcast_to(jnp.max(scores, axis=1, keepdims=True), (length, head_size))
        sums = dot(row_weights([scores], peak, rate), values)
        peak_ref[:, span] = peak
        weighted_ref[:, span] = sums[:, :head_size]
        total_ref[:, span] = sums[:, head_size:]


def first_queries(heads, *refs):
    queries_ref, both_ref, ones_ref, partial_ref, reflect_ref, gain_ref = refs[:6]
    *state_refs, solved_ref = refs[6:]
    solved = solve_rows(partial_ref, reflect_ref)
    wide_size = solved[0].shape[1]
    solved_ref[:, :wide_size] = solved[0]
    solved_ref[:, wide_size:] = solved[1]
    query_heads(heads, queries_ref, both_ref, ones_ref, solved, gain_ref, state_refs)


def other_queries(heads, longest, docs_hbm, *refs):
    queries_ref, both_ref, ones_ref, solved_ref, gain_ref = refs[:5]
    *state_refs, present_ref, docs_ref, docs_sem = refs[9:]
    docs_copy = pltpu.make_async_copy(docs_hbm, docs_ref, docs_sem)
    docs_copy.start()
    for done_ref, state_ref in zip(refs[5:9], state_refs):
        state_ref[:, : done_ref.shape[1]] = done_ref[...]
    wide_size = solved_ref.shape[1] // 2
    solved = (solved_ref[:, :wide_size], solved_ref[:, wide_size:])
    query_heads(heads, queries_ref, both_ref, ones_ref, solved, gain_ref, state_refs)
    docs_copy.wait()
    block = lax.axis_index("outer") * lax.axis_size("inner") + lax.axis_index("inner")
    own_doc = docs_ref[block]
    present = jnp.int32(0)
    for distance in range(1, longest):
        source = block - distance
        same = (source >= 0) & (docs_ref[jnp.maximum(source, 0)] == own_doc)
        present = present + same.astype(jnp.int32)
    state = 2 * present + block % 2
    present_ref[...] = jnp.full(present_ref.shape, state, jnp.int32)


def present_and_odd(present_ref):
    state = present_ref[0, 0]
    return state // 2, state % 2 == 1


def put_out(out_ref, out_hbm, out_sems, head, head_size):
    span = slice(head * head_size, (head + 1) * head_size)
    return pltpu.make_async_copy(out_ref.at[:, span], out_hbm.at[:, span], out_sems.at[head])


def attend(heads, state_refs, new_refs, all_keys, values, out_refs):
    turned_ref, peak_ref, total_ref, weighted_ref = state_refs
    head_size = values.shape[1] // 2
    rate = math.log2(math.e) * head_size ** (-0.5)
    for head in heads:
        span = slice(head * head_size, (head + 1) * head_size)
        old_peak = peak_ref[:, span]
        scores = [dot(turned_ref[:, span], keys) for keys in all_keys]
        peak = row_peak(scores, old_peak)
        sums = dot(row_weights(scores, peak, rate), values)
        factor = jnp.exp2((old_peak - peak) * rate)
        total = total_ref[:, span] * factor + sums[:, head_size:]
        weighted = weighted_ref[:, span] * factor + sums[:, :head_size]
        if out_refs is not None:
            out_refs[0][:, span] = (weighted * reciprocal(total)).astype(BF16)
            if len(out_refs) > 1:
                put_out(*out_refs, head, head_size).start()
        else:
            for new_ref, new in zip(new_refs, (peak, total, weighted)):
                new_ref[:, span] = new
    if out_refs is not None and len(out_refs) > 1:
        wait_out(heads, out_refs, head_size)


def finish(head_count, sum_refs, out_refs):
    total_ref, weighted_ref = sum_refs
    head_size = total_ref.shape[1] // head_count
    for head in range(head_count):
        span = slice(head * head_size, (head + 1) * head_size)
        out_refs[0][:, span] = (weighted_ref[:, span] * reciprocal(total_ref[:, span])).astype(BF16)
        put_out(*out_refs, head, head_size).start()
    wait_out(range(head_count), out_refs, head_size)


def wait_out(heads, out_refs, head_size):
    for head in heads:
        put_out(*out_refs, head, head_size).wait()


def store_values(values_ref, slot, place, packet, length):
    head_size = packet.shape[0]
    rows = pl.ds(place * length, length)
    start = length + head_size
    pieces = [
        packet[:, at : at + head_size] for at in range(start, start + length, head_size)
    ]
    values_ref[slot, rows, :head_size] = jnp.concatenate(pieces, axis=0)
    values_ref[slot, rows, head_size:] = jnp.ones((length, head_size), BF16)


def nearest(heads, old_refs, new_refs, packet_ref, values_ref, out_refs):
    packet = packet_ref[...]
    length = values_ref.shape[1]
    store_values(values_ref, 0, 0, packet, length)
    attend(heads, old_refs, new_refs, [packet[:, :length]], values_ref[0], out_refs)


def is_first_odd():
    return (lax.axis_index("outer") == 0) & (lax.axis_index("inner") == 1)


def early_kernel(heads, present_ref, beside_ref, *refs):
    *state_refs, done_ref, values_ref = refs
    present, _ = present_and_odd(present_ref)

    @pl.when(is_first_odd() & (present == 1))
    def _():
        nearest(heads, state_refs, None, beside_ref, values_ref, (done_ref,))


def nearest_kernel(head_count, early_heads, present_ref, beside_ref, done_ref, *refs):
    old_refs, new_refs = refs[:4], refs[4:7]
    out_hbm, out_ref, values_ref, out_sems = refs[7:]
    out_refs = (out_ref, out_hbm, out_sems)
    present, odd = present_and_odd(present_ref)
    first_odd = is_first_odd()
    heads = range(head_count)

    @pl.when(present == 0)
    def _():
        finish(head_count, old_refs[2:], out_refs)

    @pl.when(first_odd & (present == 1))
    def _():
        head_size = beside_ref.shape[0]
        done_refs = (done_ref, out_hbm, out_sems)
        for head in heads[:early_heads]:
            put_out(*done_refs, head, head_size).start()
        if early_heads < head_count:
            nearest(heads[early_heads:], old_refs, new_refs, beside_ref, values_ref, out_refs)
        wait_out(heads[:early_heads], done_refs, head_size)

    @pl.when(odd & (present == 1) & jnp.logical_not(first_odd))
    def _():
        nearest(heads, old_refs, new_refs, beside_ref, values_ref, out_refs)

    @pl.when(odd & (present > 1))
    def _():
        nearest(heads, old_refs, new_refs, beside_ref, values_ref, None)

    @pl.when(jnp.logical_not(odd) & (present > 0))
    def _():
        for old_ref, new_ref in zip(old_refs[1:], new_refs):
            new_ref[...] = old_ref[...]


def earlier_kernel(head_count, longest, present_ref, *refs):
    packet_refs = refs[:longest]
    state_refs = refs[longest : longest + 4]
    out_hbm, out_ref, keys_ref, values_ref, out_sems = refs[-5:]
    out_refs = (out_ref, out_hbm, out_sems)
    present, odd = present_and_odd(present_ref)
    length = out_ref.shape[0]
    head_size = out_ref.shape[1] // head_count
    wide_size = length + head_size
    steps = longest // 2 - 1
    apart_refs, swapped_refs = packet_refs[:steps], packet_refs[steps : 2 * steps]
    mixed_ref, beside_ref = packet_refs[2 * steps :]
    slots = values_ref.shape[0]

    def packet_of(distance, known_odd):
        if distance % 2 == 0:
            return apart_refs[distance // 2 - 1][...]
        odd_ref = beside_ref if distance == 1 else swapped_refs[(distance - 1) // 2 - 1]
        even_ref = mixed_ref if distance == longest - 1 else swapped_refs[(distance + 1) // 2 - 1]
        if known_odd is None:
            return jnp.where(odd, odd_ref[...], even_ref[...])
        return (odd_ref if known_odd else even_ref)[...]

    def collect(first, last, known_odd=None):
        transit = None
        all_keys = []
        for distance in range(1, last + 1):
            packet = packet_of(distance, known_odd)
            keys = packet[:, :length]
            own_transit = packet[:, length:wide_size]
            if distance == 1:
                transit = own_transit
            elif distance == 2:
                keys = dot(transit, keys).astype(BF16)
                if distance < last:
                    transit = dot(transit, own_transit)
            else:
                high, low = halves(transit)
                keys = (dot(high, keys) + dot(low, keys)).astype(BF16)
                if distance < last:
                    transit = dot(high, own_transit) + dot(low, own_transit)
            if distance >= first:
                all_keys.append(keys)
                index = distance - first
                store_values(values_ref, index // GROUP, index % GROUP, packet, length)
        return all_keys

    def take(first, last, known_odd):
        keys = collect(first, last, known_odd)
        values = values_ref[0, : len(keys) * length, :]
        attend(range(head_count), state_refs, None, keys, values, out_refs)

    def choose(first, last, known_odd):
        if first == last:
            take(2 if known_odd else 1, last, known_odd)
        else:
            middle = (first + last + 1) // 2
            lax.cond(
                present >= middle,
                lambda: choose(middle, last, known_odd),
                lambda: choose(first, middle - 1, known_odd),
            )

    if slots == 1:

        work = (present > odd.astype(jnp.int32)).astype(jnp.int32)

        @pl.loop(0, work)
        def _(_):
            lax.cond(
                odd,
                lambda: choose(2, longest - 1, True),
                lambda: choose(1, longest - 1, False),
            )

    else:

        @pl.when(present > 0)
        def _():
            for index, keys in enumerate(collect(1, longest - 1)):
                slot, place = index // GROUP, index % GROUP
                keys_ref[slot, :, place * length : (place + 1) * length] = keys

        def visit(slot, blocks):
            keys = [keys_ref[slot, :, i * length : (i + 1) * length] for i in range(blocks)]
            values = values_ref[slot, : blocks * length, :]
            attend(range(head_count), state_refs, state_refs[1:], keys, values, None)

        full = present // GROUP

        @pl.loop(0, full)
        def _(slot):
            visit(slot, GROUP)

        for blocks in range(1, GROUP):
            pl.when(present % GROUP == blocks)(functools.partial(visit, full, blocks))
        finish(head_count, state_refs[2:], out_refs)


def vmem(count):
    return [pl.BlockSpec(memory_space=pltpu.VMEM)] * count


def in_hbm(value):
    return pltpu.with_memory_space_constraint(value, pltpu.HBM)


def permuted(value, target):
    count = lax.axis_size("outer") * lax.axis_size("inner")
    return lax.ppermute(value, AXES, [(i, target(i) % count) for i in range(count)])


def local(queries, keys, values, reflect, reflect_logit, doc_of_block):
    longest = lax.axis_size("outer") * lax.axis_size("inner") // 8
    length, head_size = keys.shape
    head_count = queries.shape[1] // head_size
    wide_size = length + head_size
    params = pltpu.CompilerParams(vmem_limit_bytes=VMEM_LIMIT)
    shape = jax.ShapeDtypeStruct
    hbm = pl.BlockSpec(memory_space=pltpu.HBM)
    packet, partial, gain, both, ones, reflect_rows = pl.pallas_call(
        key_kernel,
        out_shape=(
            shape((head_size, wide_size + length), BF16),
            shape((length // 2, 3 * length), F32),
            shape((8, length), F32),
            shape((head_size, 2 * length), BF16),
            shape((length, 2 * head_size), BF16),
            shape((length, head_size), BF16),
        ),
        in_specs=[hbm] * 4,
        out_specs=tuple(vmem(6)),
        scratch_shapes=[
            pltpu.VMEM((length, head_size), BF16),
            pltpu.VMEM((1, length), F32),
            pltpu.SemaphoreType.DMA((4,)),
        ],
        compiler_params=params,
        cost_estimate=pl.CostEstimate(
            flops=40 * length**3, bytes_accessed=8 * length * length, transcendentals=length
        ),
        name="key_side",
    )(*(in_hbm(value) for value in (reflect, keys, values, reflect_logit.reshape(1, length))))
    apart = [permuted(packet, lambda i, s=s: i + 2 * s) for s in range(1, longest // 2)]
    wide = shape(queries.shape, F32)
    state_shapes = (shape(queries.shape, BF16), wide, wide, wide)
    first = max(1, head_count // 4)
    first_shapes = [shape((length, first * head_size), part.dtype) for part in state_shapes]

    def query_cost(heads):
        return pl.CostEstimate(
            flops=heads * 10 * length**3,
            bytes_accessed=16 * length * length * heads,
            transcendentals=heads * length * length,
        )

    *state, solved = pl.pallas_call(
        functools.partial(first_queries, range(first)),
        out_shape=(*first_shapes, shape((length, 2 * wide_size), BF16)),
        in_specs=vmem(6),
        out_specs=tuple(vmem(5)),
        compiler_params=params,
        cost_estimate=query_cost(first),
        name="first_queries",
    )(queries, both, ones, partial, reflect_rows, gain)
    mixed_packet, state[0] = lax.optimization_barrier((packet, state[0]))
    beside = permuted(mixed_packet, lambda i: i ^ 1)
    mixed = permuted(mixed_packet, lambda i: i + longest - 1 if i % 2 else i + 1)
    slots = (longest - 1 + GROUP - 1) // GROUP
    one_values = pltpu.VMEM((1, length, 2 * head_size), BF16)
    *state, present = pl.pallas_call(
        functools.partial(other_queries, range(first, head_count), longest),
        out_shape=(*state_shapes, shape((8, 128), jnp.int32)),
        in_specs=[hbm] + vmem(9),
        out_specs=tuple(vmem(5)),
        scratch_shapes=[
            pltpu.SMEM(doc_of_block.shape, jnp.int32),
            pltpu.SemaphoreType.DMA(()),
        ],
        compiler_params=params,
        cost_estimate=query_cost(head_count - first),
        name="other_queries",
    )(in_hbm(doc_of_block), queries, both, ones, solved, gain, *state)
    out_shape = shape(queries.shape, BF16)
    slots = (longest - 1 + GROUP - 1) // GROUP
    one_values = pltpu.VMEM((1, length, 2 * head_size), BF16)
    out_scratch = [pltpu.VMEM(queries.shape, BF16), pltpu.SemaphoreType.DMA((head_count,))]
    nearest_cost = pl.CostEstimate(
        flops=head_count * 2 * length**3,
        bytes_accessed=4 * length * length * head_count,
        transcendentals=head_count * length * length,
    )
    turned = state[0]
    *apart, present = lax.optimization_barrier((*apart, present))
    early_heads = max(1, 5 * head_count // 8)
    if slots == 1:
        done = pl.pallas_call(
            functools.partial(early_kernel, range(early_heads)),
            out_shape=shape((length, early_heads * head_size), BF16),
            in_specs=vmem(6),
            out_specs=vmem(1)[0],
            scratch_shapes=[one_values],
            compiler_params=params,
            cost_estimate=pl.CostEstimate(flops=0, bytes_accessed=0, transcendentals=0),
            name="early_heads",
        )(present, beside, *state)
        *apart, done = lax.optimization_barrier((*apart, done))
    swapped = [permuted(moved, lambda i: i ^ 1) for moved in apart]
    sums, started = state[1:], []
    if slots == 1:
        *sums, out = pl.pallas_call(
            functools.partial(nearest_kernel, head_count, early_heads),
            out_shape=(*state_shapes[1:], out_shape),
            in_specs=vmem(7),
            out_specs=(*vmem(3), hbm),
            scratch_shapes=[out_scratch[0], one_values, out_scratch[1]],
            compiler_params=params,
            cost_estimate=nearest_cost,
            name="nearest_block",
        )(present, beside, done, *state)
        started = [in_hbm(out)]
    return pl.pallas_call(
        functools.partial(earlier_kernel, head_count, longest),
        out_shape=out_shape,
        in_specs=vmem(longest + 5) + [hbm] * len(started),
        out_specs=hbm,
        input_output_aliases={longest + 5: 0} if started else {},
        scratch_shapes=[
            out_scratch[0],
            pltpu.VMEM((slots, head_size, GROUP * length), BF16),
            pltpu.VMEM((slots, GROUP * length, 2 * head_size), BF16),
            out_scratch[1],
        ],
        compiler_params=params,
        cost_estimate=pl.CostEstimate(
            flops=head_count * 6 * length**3,
            bytes_accessed=16 * length * length * head_count,
            transcendentals=3 * head_count * length * length,
        ),
        name="earlier_blocks",
    )(present, *apart, *swapped, mixed, beside, turned, *sums, *started)


def solution(mesh):
    placed = (
        P(AXES, None),
        P(AXES, None),
        P(AXES, None),
        P(AXES, None),
        P(AXES),
        P(),
    )
    return jax.shard_map(
        local, mesh=mesh, in_specs=placed, out_specs=P(AXES, None), check_vma=False
    )
```

```python
import functools
import math

import jax
import jax.numpy as jnp
from jax import lax
from jax.experimental import pallas as pl
from jax.experimental.pallas import tpu as pltpu
from jax.sharding import PartitionSpec as P

F32 = jnp.float32
BF16 = jnp.bfloat16
AXES = ("outer", "inner")
GROUP = 3
VMEM_LIMIT = 24 * 1024 * 1024


def dot(left, right):
    return jnp.dot(left, right, preferred_element_type=F32)


def dot_rows(left, right):
    return lax.dot_general(left, right, (((1,), (1,)), ((), ())), preferred_element_type=F32)


def halves(value):
    high = value.astype(BF16)
    return high, (value - high.astype(F32)).astype(BF16)


def dot_halves(left, right):
    (left_high, left_low), (right_high, right_low) = left, right
    return dot(left_high, right_high) + (dot(left_high, right_low) + dot(left_low, right_high))


def dot_joined(left, right):
    (left_high, left_low), (right_high, right_low) = left, right
    return dot(
        jnp.concatenate([left_high, left_low, left_high], axis=1),
        jnp.concatenate([right_high, right_high, right_low], axis=0),
    )


def unit_inverses(strict_parts):
    length = strict_parts[0].shape[0]
    rows = lax.broadcasted_iota(jnp.int32, (length, length), 0)
    columns = lax.broadcasted_iota(jnp.int32, (length, length), 1)
    identity = (rows == columns).astype(F32)
    results = [identity - part for part in strict_parts]
    powers = list(strict_parts)
    reach = 2
    while reach < length:
        for index, (result, power) in enumerate(zip(results, powers)):
            power = halves(power)
            powers[index] = dot_joined(power, power)
            if reach > 2:
                results[index] = result + dot_joined(halves(result), power)
        reach = reach * 2
    return [
        result + dot_joined(halves(result), halves(power))
        for result, power in zip(results, powers)
    ]


def key_kernel(
    reflect_hbm,
    keys_hbm,
    values_hbm,
    logit_hbm,
    packet_ref,
    partial_ref,
    gain_ref,
    turned_ref,
    ones_ref,
    reflect_ref,
    keys_ref,
    logit_ref,
    sems,
):
    length, head_size = reflect_ref.shape
    half = length // 2
    wide_size = length + head_size
    copies = [
        pltpu.make_async_copy(reflect_hbm, reflect_ref, sems.at[0]),
        pltpu.make_async_copy(logit_hbm, logit_ref, sems.at[1]),
        pltpu.make_async_copy(keys_hbm, keys_ref, sems.at[2]),
        pltpu.make_async_copy(values_hbm, ones_ref.at[:, pl.ds(0, head_size)], sems.at[3]),
    ]
    for copy in copies:
        copy.start()
    copies[0].wait()
    copies[1].wait()
    reflect = reflect_ref[...]
    reflect_float = reflect.astype(F32)
    square_high, square_low = halves(reflect_float * reflect_float)
    ones = jnp.ones((8, head_size), BF16)
    norms = dot_rows(ones, square_high) + dot_rows(ones, square_low)
    strength = 2.0 / (1.0 + jnp.exp(-logit_ref[...]))
    gains = strength / (norms + 1e-06)
    gain_ref[...] = gains
    gain = gains[0:1, :]
    rows = lax.broadcasted_iota(jnp.int32, (length, length), 0)
    columns = lax.broadcasted_iota(jnp.int32, (length, length), 1)
    strictly = rows > columns
    chained = jnp.where(strictly, dot_rows(reflect, reflect) * gain, 0.0)
    copies[2].wait()
    keys = keys_ref[...]
    facing = jnp.where(strictly, dot_rows(reflect, keys), 0.0)
    reflect_turned = reflect_float.T
    keys_turned = keys.astype(F32).T
    turned_ref[:, :length] = reflect_turned.astype(BF16)
    turned_ref[:, length:] = keys_turned.astype(BF16)
    scaled_high, scaled_low = halves(reflect_turned * gain)
    scaled_first = (scaled_high[:, :half], scaled_low[:, :half])
    scaled_second = (scaled_high[:, half:], scaled_low[:, half:])
    across = halves(chained[half:, :half])
    wide = halves(jnp.concatenate([facing[:half, :half], reflect_float[:half]], axis=1))
    tall = halves(
        jnp.concatenate([facing[half:, :half], reflect_float[half:], facing[half:, half:]], axis=1)
    )
    first, second = unit_inverses([chained[:half, :half], chained[half:, half:]])
    upper = dot_joined(halves(first), wide)
    reach = halves(dot_joined(scaled_second, halves(second)))
    bridge = dot_joined(reach, across)
    upper_halves = halves(upper)
    own = dot_joined(scaled_first, upper_halves)
    later = dot_joined(reach, tall)
    change = (own + later[:, :wide_size - half]) - dot_joined(halves(bridge), upper_halves)
    partial_ref[:, :half] = second
    partial_ref[:, half:length] = chained[half:, :half]
    partial_ref[:, length : 2 * length] = facing[half:, :]
    partial_ref[:, 2 * length :] = upper
    head_rows = lax.broadcasted_iota(jnp.int32, (head_size, head_size), 0)
    head_columns = lax.broadcasted_iota(jnp.int32, (head_size, head_size), 1)
    identity = (head_rows == head_columns).astype(F32)
    packet_ref[:, :half] = (keys_turned[:, :half] - change[:, :half]).astype(BF16)
    packet_ref[:, half:length] = (keys_turned[:, half:] - later[:, half + head_size :]).astype(BF16)
    packet_ref[:, length:wide_size] = (identity - change[:, half:]).astype(BF16)
    copies[3].wait()
    ones_ref[:, head_size:] = jnp.ones((length, head_size), BF16)
    for part in range(length // head_size):
        start = wide_size + part * head_size
        packet_ref[:, start : start + head_size] = ones_ref[
            part * head_size : (part + 1) * head_size, :head_size
        ]


def solve_rows(partial_ref, reflect_ref):
    length, head_size = reflect_ref.shape
    half = length // 2
    second = halves(partial_ref[:, :half])
    across = halves(partial_ref[:, half:length])
    facing = partial_ref[:, length : 2 * length]
    upper = partial_ref[:, 2 * length :]
    reflect = reflect_ref[half:, :].astype(F32)
    tall = jnp.concatenate([facing[:, :half], reflect, facing[:, half:]], axis=1)
    lower = dot_halves(second, halves(tall))
    bridge = dot_halves(second, across)
    lower_left = lower[:, : half + head_size] - dot_halves(halves(bridge), halves(upper))
    top = [upper[:, :half], jnp.zeros((half, half), F32), upper[:, half:]]
    bottom = [lower_left[:, :half], lower[:, half + head_size :], lower_left[:, half:]]
    return halves(
        jnp.concatenate([jnp.concatenate(top, axis=1), jnp.concatenate(bottom, axis=1)], axis=0)
    )


def lane_pieces(scores, size):
    return [score[:, i : i + size] for score in scores for i in range(0, score.shape[1], size)]


def row_peak(scores, peak):
    largest = functools.reduce(jnp.maximum, lane_pieces(scores, peak.shape[1]))
    return jnp.maximum(peak, jnp.max(largest, axis=1, keepdims=True))


def row_weights(scores, peak, rate):
    pieces = [jnp.exp2((piece - peak) * rate) for piece in lane_pieces(scores, peak.shape[1])]
    return jnp.concatenate(pieces, axis=1).astype(BF16)


def reciprocal(value):
    rough = pl.reciprocal(value, approx=True)
    return rough * (2.0 - value * rough)


def query_heads(heads, queries_ref, both_ref, ones_ref, solved, gain_ref, state_refs):
    turned_ref, peak_ref, total_ref, weighted_ref = state_refs
    length = ones_ref.shape[0]
    head_size = ones_ref.shape[1] // 2
    rate = math.log2(math.e) * head_size ** (-0.5)
    rows = lax.broadcasted_iota(jnp.int32, (length, length), 0)
    columns = lax.broadcasted_iota(jnp.int32, (length, length), 1)
    visible = rows >= columns
    gain = jnp.where(visible, gain_ref[0:1, :], 0.0)
    hidden = jnp.where(visible, 0.0, -1e30)
    both = both_ref[...]
    values = ones_ref[...]
    for head in heads:
        span = slice(head * head_size, (head + 1) * head_size)
        queries = queries_ref[:, span]
        faced = dot(queries, both)
        change = dot_halves(halves(faced[:, :length] * gain), solved)
        scores = (faced[:, length:] - change[:, :length]) + hidden
        turned_ref[:, span] = (queries.astype(F32) - change[:, length:]).astype(BF16)
        peak = jnp.broadcast_to(jnp.max(scores, axis=1, keepdims=True), (length, head_size))
        sums = dot(row_weights([scores], peak, rate), values)
        peak_ref[:, span] = peak
        weighted_ref[:, span] = sums[:, :head_size]
        total_ref[:, span] = sums[:, head_size:]


def first_queries(heads, *refs):
    queries_ref, both_ref, ones_ref, partial_ref, reflect_ref, gain_ref = refs[:6]
    *state_refs, solved_ref = refs[6:]
    solved = solve_rows(partial_ref, reflect_ref)
    wide_size = solved[0].shape[1]
    solved_ref[:, :wide_size] = solved[0]
    solved_ref[:, wide_size:] = solved[1]
    query_heads(heads, queries_ref, both_ref, ones_ref, solved, gain_ref, state_refs)


def other_queries(heads, longest, docs_hbm, *refs):
    queries_ref, both_ref, ones_ref, solved_ref, gain_ref = refs[:5]
    *state_refs, present_ref, docs_ref, docs_sem = refs[9:]
    docs_copy = pltpu.make_async_copy(docs_hbm, docs_ref, docs_sem)
    docs_copy.start()
    for done_ref, state_ref in zip(refs[5:9], state_refs):
        state_ref[:, : done_ref.shape[1]] = done_ref[...]
    wide_size = solved_ref.shape[1] // 2
    solved = (solved_ref[:, :wide_size], solved_ref[:, wide_size:])
    query_heads(heads, queries_ref, both_ref, ones_ref, solved, gain_ref, state_refs)
    docs_copy.wait()
    block = lax.axis_index("outer") * lax.axis_size("inner") + lax.axis_index("inner")
    own_doc = docs_ref[block]
    present = jnp.int32(0)
    for distance in range(1, longest):
        source = block - distance
        same = (source >= 0) & (docs_ref[jnp.maximum(source, 0)] == own_doc)
        present = present + same.astype(jnp.int32)
    state = 2 * present + block % 2
    present_ref[...] = jnp.full(present_ref.shape, state, jnp.int32)


def present_and_odd(present_ref):
    state = present_ref[0, 0]
    return state // 2, state % 2 == 1


def put_out(out_ref, out_hbm, out_sems, head, head_size):
    span = slice(head * head_size, (head + 1) * head_size)
    return pltpu.make_async_copy(out_ref.at[:, span], out_hbm.at[:, span], out_sems.at[head])


def attend(heads, state_refs, new_refs, all_keys, values, out_refs):
    turned_ref, peak_ref, total_ref, weighted_ref = state_refs
    head_size = values.shape[1] // 2
    rate = math.log2(math.e) * head_size ** (-0.5)
    for head in heads:
        span = slice(head * head_size, (head + 1) * head_size)
        old_peak = peak_ref[:, span]
        scores = [dot(turned_ref[:, span], keys) for keys in all_keys]
        peak = row_peak(scores, old_peak)
        sums = dot(row_weights(scores, peak, rate), values)
        factor = jnp.exp2((old_peak - peak) * rate)
        total = total_ref[:, span] * factor + sums[:, head_size:]
        weighted = weighted_ref[:, span] * factor + sums[:, :head_size]
        if out_refs is not None:
            out_refs[0][:, span] = (weighted * reciprocal(total)).astype(BF16)
            if len(out_refs) > 1:
                put_out(*out_refs, head, head_size).start()
        else:
            for new_ref, new in zip(new_refs, (peak, total, weighted)):
                new_ref[:, span] = new
    if out_refs is not None and len(out_refs) > 1:
        wait_out(heads, out_refs, head_size)


def finish(head_count, sum_refs, out_refs):
    total_ref, weighted_ref = sum_refs
    head_size = total_ref.shape[1] // head_count
    for head in range(head_count):
        span = slice(head * head_size, (head + 1) * head_size)
        out_refs[0][:, span] = (weighted_ref[:, span] * reciprocal(total_ref[:, span])).astype(BF16)
        put_out(*out_refs, head, head_size).start()
    wait_out(range(head_count), out_refs, head_size)


def wait_out(heads, out_refs, head_size):
    for head in heads:
        put_out(*out_refs, head, head_size).wait()


def store_values(values_ref, slot, place, packet, length):
    head_size = packet.shape[0]
    rows = pl.ds(place * length, length)
    start = length + head_size
    pieces = [
        packet[:, at : at + head_size] for at in range(start, start + length, head_size)
    ]
    values_ref[slot, rows, :head_size] = jnp.concatenate(pieces, axis=0)
    values_ref[slot, rows, head_size:] = jnp.ones((length, head_size), BF16)


def nearest(heads, old_refs, new_refs, packet_ref, values_ref, out_refs):
    packet = packet_ref[...]
    length = values_ref.shape[1]
    store_values(values_ref, 0, 0, packet, length)
    attend(heads, old_refs, new_refs, [packet[:, :length]], values_ref[0], out_refs)


def is_first_odd():
    return (lax.axis_index("outer") == 0) & (lax.axis_index("inner") == 1)


def early_kernel(heads, present_ref, beside_ref, *refs):
    *state_refs, done_ref, values_ref = refs
    present, _ = present_and_odd(present_ref)

    @pl.when(is_first_odd() & (present == 1))
    def _():
        nearest(heads, state_refs, None, beside_ref, values_ref, (done_ref,))


def nearest_kernel(head_count, early_heads, present_ref, beside_ref, done_ref, *refs):
    old_refs, new_refs = refs[:4], refs[4:7]
    out_hbm, out_ref, values_ref, out_sems = refs[7:]
    out_refs = (out_ref, out_hbm, out_sems)
    present, odd = present_and_odd(present_ref)
    first_odd = is_first_odd()
    heads = range(head_count)

    @pl.when(present == 0)
    def _():
        finish(head_count, old_refs[2:], out_refs)

    @pl.when(first_odd & (present == 1))
    def _():
        head_size = beside_ref.shape[0]
        done_refs = (done_ref, out_hbm, out_sems)
        for head in heads[:early_heads]:
            put_out(*done_refs, head, head_size).start()
        if early_heads < head_count:
            nearest(heads[early_heads:], old_refs, new_refs, beside_ref, values_ref, out_refs)
        wait_out(heads[:early_heads], done_refs, head_size)

    @pl.when(odd & (present == 1) & jnp.logical_not(first_odd))
    def _():
        nearest(heads, old_refs, new_refs, beside_ref, values_ref, out_refs)

    @pl.when(odd & (present > 1))
    def _():
        nearest(heads, old_refs, new_refs, beside_ref, values_ref, None)

    @pl.when(jnp.logical_not(odd) & (present > 0))
    def _():
        for old_ref, new_ref in zip(old_refs[1:], new_refs):
            new_ref[...] = old_ref[...]


def earlier_kernel(head_count, longest, present_ref, *refs):
    packet_refs = refs[:longest]
    state_refs = refs[longest : longest + 4]
    out_hbm, out_ref, keys_ref, values_ref, out_sems = refs[-5:]
    out_refs = (out_ref, out_hbm, out_sems)
    present, odd = present_and_odd(present_ref)
    length = out_ref.shape[0]
    head_size = out_ref.shape[1] // head_count
    wide_size = length + head_size
    steps = longest // 2 - 1
    apart_refs, swapped_refs = packet_refs[:steps], packet_refs[steps : 2 * steps]
    mixed_ref, beside_ref = packet_refs[2 * steps :]
    slots = values_ref.shape[0]

    def packet_of(distance, known_odd):
        if distance % 2 == 0:
            return apart_refs[distance // 2 - 1][...]
        odd_ref = beside_ref if distance == 1 else swapped_refs[(distance - 1) // 2 - 1]
        even_ref = mixed_ref if distance == longest - 1 else swapped_refs[(distance + 1) // 2 - 1]
        if known_odd is None:
            return jnp.where(odd, odd_ref[...], even_ref[...])
        return (odd_ref if known_odd else even_ref)[...]

    def collect(first, last, known_odd=None):
        transit = None
        all_keys = []
        for distance in range(1, last + 1):
            packet = packet_of(distance, known_odd)
            keys = packet[:, :length]
            own_transit = packet[:, length:wide_size]
            if distance == 1:
                transit = own_transit
            elif distance == 2:
                keys = dot(transit, keys).astype(BF16)
                if distance < last:
                    transit = dot(transit, own_transit)
            else:
                high, low = halves(transit)
                keys = (dot(high, keys) + dot(low, keys)).astype(BF16)
                if distance < last:
                    transit = dot(high, own_transit) + dot(low, own_transit)
            if distance >= first:
                all_keys.append(keys)
                index = distance - first
                store_values(values_ref, index // GROUP, index % GROUP, packet, length)
        return all_keys

    def take(first, last, known_odd):
        keys = collect(first, last, known_odd)
        values = values_ref[0, : len(keys) * length, :]
        attend(range(head_count), state_refs, None, keys, values, out_refs)

    def choose(first, last, known_odd):
        if first == last:
            take(2 if known_odd else 1, last, known_odd)
        else:
            middle = (first + last + 1) // 2
            lax.cond(
                present >= middle,
                lambda: choose(middle, last, known_odd),
                lambda: choose(first, middle - 1, known_odd),
            )

    if slots == 1:

        work = (present > odd.astype(jnp.int32)).astype(jnp.int32)

        @pl.loop(0, work)
        def _(_):
            lax.cond(
                odd,
                lambda: choose(2, longest - 1, True),
                lambda: choose(1, longest - 1, False),
            )

    else:

        @pl.when(present > 0)
        def _():
            for index, keys in enumerate(collect(1, longest - 1)):
                slot, place = index // GROUP, index % GROUP
                keys_ref[slot, :, place * length : (place + 1) * length] = keys

        def visit(slot, blocks):
            keys = [keys_ref[slot, :, i * length : (i + 1) * length] for i in range(blocks)]
            values = values_ref[slot, : blocks * length, :]
            attend(range(head_count), state_refs, state_refs[1:], keys, values, None)

        full = present // GROUP

        @pl.loop(0, full)
        def _(slot):
            visit(slot, GROUP)

        for blocks in range(1, GROUP):
            pl.when(present % GROUP == blocks)(functools.partial(visit, full, blocks))
        finish(head_count, state_refs[2:], out_refs)


def vmem(count):
    return [pl.BlockSpec(memory_space=pltpu.VMEM)] * count


def in_hbm(value):
    return pltpu.with_memory_space_constraint(value, pltpu.HBM)


def permuted(value, target):
    count = lax.axis_size("outer") * lax.axis_size("inner")
    return lax.ppermute(value, AXES, [(i, target(i) % count) for i in range(count)])


def local(queries, keys, values, reflect, reflect_logit, doc_of_block):
    longest = lax.axis_size("outer") * lax.axis_size("inner") // 8
    length, head_size = keys.shape
    head_count = queries.shape[1] // head_size
    wide_size = length + head_size
    params = pltpu.CompilerParams(vmem_limit_bytes=VMEM_LIMIT)
    shape = jax.ShapeDtypeStruct
    hbm = pl.BlockSpec(memory_space=pltpu.HBM)
    packet, partial, gain, both, ones, reflect_rows = pl.pallas_call(
        key_kernel,
        out_shape=(
            shape((head_size, wide_size + length), BF16),
            shape((length // 2, 3 * length), F32),
            shape((8, length), F32),
            shape((head_size, 2 * length), BF16),
            shape((length, 2 * head_size), BF16),
            shape((length, head_size), BF16),
        ),
        in_specs=[hbm] * 4,
        out_specs=tuple(vmem(6)),
        scratch_shapes=[
            pltpu.VMEM((length, head_size), BF16),
            pltpu.VMEM((1, length), F32),
            pltpu.SemaphoreType.DMA((4,)),
        ],
        compiler_params=params,
        cost_estimate=pl.CostEstimate(
            flops=40 * length**3, bytes_accessed=8 * length * length, transcendentals=length
        ),
        name="key_side",
    )(*(in_hbm(value) for value in (reflect, keys, values, reflect_logit.reshape(1, length))))
    apart = [permuted(packet, lambda i, s=s: i + 2 * s) for s in range(1, longest // 2)]
    wide = shape(queries.shape, F32)
    state_shapes = (shape(queries.shape, BF16), wide, wide, wide)
    first = max(1, head_count // 4)
    first_shapes = [shape((length, first * head_size), part.dtype) for part in state_shapes]

    def query_cost(heads):
        return pl.CostEstimate(
            flops=heads * 10 * length**3,
            bytes_accessed=16 * length * length * heads,
            transcendentals=heads * length * length,
        )

    *state, solved = pl.pallas_call(
        functools.partial(first_queries, range(first)),
        out_shape=(*first_shapes, shape((length, 2 * wide_size), BF16)),
        in_specs=vmem(6),
        out_specs=tuple(vmem(5)),
        compiler_params=params,
        cost_estimate=query_cost(first),
        name="first_queries",
    )(queries, both, ones, partial, reflect_rows, gain)
    mixed_packet, state[0] = lax.optimization_barrier((packet, state[0]))
    beside = permuted(mixed_packet, lambda i: i ^ 1)
    mixed = permuted(mixed_packet, lambda i: i + longest - 1 if i % 2 else i + 1)
    slots = (longest - 1 + GROUP - 1) // GROUP
    one_values = pltpu.VMEM((1, length, 2 * head_size), BF16)
    *state, present = pl.pallas_call(
        functools.partial(other_queries, range(first, head_count), longest),
        out_shape=(*state_shapes, shape((8, 128), jnp.int32)),
        in_specs=[hbm] + vmem(9),
        out_specs=tuple(vmem(5)),
        scratch_shapes=[
            pltpu.SMEM(doc_of_block.shape, jnp.int32),
            pltpu.SemaphoreType.DMA(()),
        ],
        compiler_params=params,
        cost_estimate=query_cost(head_count - first),
        name="other_queries",
    )(in_hbm(doc_of_block), queries, both, ones, solved, gain, *state)
    out_shape = shape(queries.shape, BF16)
    slots = (longest - 1 + GROUP - 1) // GROUP
    one_values = pltpu.VMEM((1, length, 2 * head_size), BF16)
    out_scratch = [pltpu.VMEM(queries.shape, BF16), pltpu.SemaphoreType.DMA((head_count,))]
    nearest_cost = pl.CostEstimate(
        flops=head_count * 2 * length**3,
        bytes_accessed=4 * length * length * head_count,
        transcendentals=head_count * length * length,
    )
    turned = state[0]
    *apart, present = lax.optimization_barrier((*apart, present))
    early_heads = max(1, 3 * head_count // 4)
    if slots == 1:
        done = pl.pallas_call(
            functools.partial(early_kernel, range(early_heads)),
            out_shape=shape((length, early_heads * head_size), BF16),
            in_specs=vmem(6),
            out_specs=vmem(1)[0],
            scratch_shapes=[one_values],
            compiler_params=params,
            cost_estimate=pl.CostEstimate(flops=0, bytes_accessed=0, transcendentals=0),
            name="early_heads",
        )(present, beside, *state)
        *apart, done = lax.optimization_barrier((*apart, done))
    swapped = [permuted(moved, lambda i: i ^ 1) for moved in apart]
    sums, started = state[1:], []
    if slots == 1:
        *sums, out = pl.pallas_call(
            functools.partial(nearest_kernel, head_count, early_heads),
            out_shape=(*state_shapes[1:], out_shape),
            in_specs=vmem(7),
            out_specs=(*vmem(3), hbm),
            scratch_shapes=[out_scratch[0], one_values, out_scratch[1]],
            compiler_params=params,
            cost_estimate=nearest_cost,
            name="nearest_block",
        )(present, beside, done, *state)
        started = [in_hbm(out)]
    return pl.pallas_call(
        functools.partial(earlier_kernel, head_count, longest),
        out_shape=out_shape,
        in_specs=vmem(longest + 5) + [hbm] * len(started),
        out_specs=hbm,
        input_output_aliases={longest + 5: 0} if started else {},
        scratch_shapes=[
            out_scratch[0],
            pltpu.VMEM((slots, head_size, GROUP * length), BF16),
            pltpu.VMEM((slots, GROUP * length, 2 * head_size), BF16),
            out_scratch[1],
        ],
        compiler_params=params,
        cost_estimate=pl.CostEstimate(
            flops=head_count * 6 * length**3,
            bytes_accessed=16 * length * length * head_count,
            transcendentals=3 * head_count * length * length,
        ),
        name="earlier_blocks",
    )(present, *apart, *swapped, mixed, beside, turned, *sums, *started)


def solution(mesh):
    placed = (
        P(AXES, None),
        P(AXES, None),
        P(AXES, None),
        P(AXES, None),
        P(AXES),
        P(),
    )
    return jax.shard_map(
        local, mesh=mesh, in_specs=placed, out_specs=P(AXES, None), check_vma=False
    )
```

```python
import functools
import math

import jax
import jax.numpy as jnp
from jax import lax
from jax.experimental import pallas as pl
from jax.experimental.pallas import tpu as pltpu
from jax.sharding import PartitionSpec as P

F32 = jnp.float32
BF16 = jnp.bfloat16
AXES = ("outer", "inner")
GROUP = 3
VMEM_LIMIT = 24 * 1024 * 1024


def dot(left, right):
    return jnp.dot(left, right, preferred_element_type=F32)


def dot_rows(left, right):
    return lax.dot_general(left, right, (((1,), (1,)), ((), ())), preferred_element_type=F32)


def halves(value):
    high = value.astype(BF16)
    return high, (value - high.astype(F32)).astype(BF16)


def dot_halves(left, right):
    (left_high, left_low), (right_high, right_low) = left, right
    return dot(left_high, right_high) + (dot(left_high, right_low) + dot(left_low, right_high))


def dot_joined(left, right):
    (left_high, left_low), (right_high, right_low) = left, right
    return dot(
        jnp.concatenate([left_high, left_low, left_high], axis=1),
        jnp.concatenate([right_high, right_high, right_low], axis=0),
    )


def unit_inverses(strict_parts):
    length = strict_parts[0].shape[0]
    rows = lax.broadcasted_iota(jnp.int32, (length, length), 0)
    columns = lax.broadcasted_iota(jnp.int32, (length, length), 1)
    identity = (rows == columns).astype(F32)
    results = [identity - part for part in strict_parts]
    powers = list(strict_parts)
    reach = 2
    while reach < length:
        for index, (result, power) in enumerate(zip(results, powers)):
            power = halves(power)
            powers[index] = dot_joined(power, power)
            if reach > 2:
                results[index] = result + dot_joined(halves(result), power)
        reach = reach * 2
    return [
        result + dot_joined(halves(result), halves(power))
        for result, power in zip(results, powers)
    ]


def key_kernel(
    reflect_hbm,
    keys_hbm,
    values_hbm,
    logit_hbm,
    packet_ref,
    partial_ref,
    gain_ref,
    turned_ref,
    ones_ref,
    reflect_ref,
    keys_ref,
    logit_ref,
    sems,
):
    length, head_size = reflect_ref.shape
    half = length // 2
    wide_size = length + head_size
    copies = [
        pltpu.make_async_copy(reflect_hbm, reflect_ref, sems.at[0]),
        pltpu.make_async_copy(logit_hbm, logit_ref, sems.at[1]),
        pltpu.make_async_copy(keys_hbm, keys_ref, sems.at[2]),
        pltpu.make_async_copy(values_hbm, ones_ref.at[:, pl.ds(0, head_size)], sems.at[3]),
    ]
    for copy in copies:
        copy.start()
    copies[0].wait()
    copies[1].wait()
    reflect = reflect_ref[...]
    reflect_float = reflect.astype(F32)
    square_high, square_low = halves(reflect_float * reflect_float)
    ones = jnp.ones((8, head_size), BF16)
    norms = dot_rows(ones, square_high) + dot_rows(ones, square_low)
    strength = 2.0 / (1.0 + jnp.exp(-logit_ref[...]))
    gains = strength / (norms + 1e-06)
    gain_ref[...] = gains
    gain = gains[0:1, :]
    rows = lax.broadcasted_iota(jnp.int32, (length, length), 0)
    columns = lax.broadcasted_iota(jnp.int32, (length, length), 1)
    strictly = rows > columns
    chained = jnp.where(strictly, dot_rows(reflect, reflect) * gain, 0.0)
    copies[2].wait()
    copies[3].wait()
    ones_ref[:, head_size:] = jnp.ones((length, head_size), BF16)
    for part in range(length // head_size):
        start = wide_size + part * head_size
        packet_ref[:, start : start + head_size] = ones_ref[
            part * head_size : (part + 1) * head_size, :head_size
        ]
    keys = keys_ref[...]
    facing = jnp.where(strictly, dot_rows(reflect, keys), 0.0)
    reflect_turned = reflect_float.T
    keys_turned = keys.astype(F32).T
    turned_ref[:, :length] = reflect_turned.astype(BF16)
    turned_ref[:, length:] = keys_turned.astype(BF16)
    scaled_high, scaled_low = halves(reflect_turned * gain)
    scaled_first = (scaled_high[:, :half], scaled_low[:, :half])
    scaled_second = (scaled_high[:, half:], scaled_low[:, half:])
    across = halves(chained[half:, :half])
    wide = halves(jnp.concatenate([facing[:half, :half], reflect_float[:half]], axis=1))
    tall = halves(
        jnp.concatenate([facing[half:, :half], reflect_float[half:], facing[half:, half:]], axis=1)
    )
    first, second = unit_inverses([chained[:half, :half], chained[half:, half:]])
    upper = dot_joined(halves(first), wide)
    reach = halves(dot_joined(scaled_second, halves(second)))
    bridge = dot_joined(reach, across)
    upper_halves = halves(upper)
    own = dot_joined(scaled_first, upper_halves)
    later = dot_joined(reach, tall)
    change = (own + later[:, :wide_size - half]) - dot_joined(halves(bridge), upper_halves)
    partial_ref[:, :half] = second
    partial_ref[:, half:length] = chained[half:, :half]
    partial_ref[:, length : 2 * length] = facing[half:, :]
    partial_ref[:, 2 * length :] = upper
    head_rows = lax.broadcasted_iota(jnp.int32, (head_size, head_size), 0)
    head_columns = lax.broadcasted_iota(jnp.int32, (head_size, head_size), 1)
    identity = (head_rows == head_columns).astype(F32)
    packet_ref[:, :half] = (keys_turned[:, :half] - change[:, :half]).astype(BF16)
    packet_ref[:, half:length] = (keys_turned[:, half:] - later[:, half + head_size :]).astype(BF16)
    packet_ref[:, length:wide_size] = (identity - change[:, half:]).astype(BF16)


def solve_rows(partial_ref, reflect_ref):
    length, head_size = reflect_ref.shape
    half = length // 2
    second = halves(partial_ref[:, :half])
    across = halves(partial_ref[:, half:length])
    facing = partial_ref[:, length : 2 * length]
    upper = partial_ref[:, 2 * length :]
    reflect = reflect_ref[half:, :].astype(F32)
    tall = jnp.concatenate([facing[:, :half], reflect, facing[:, half:]], axis=1)
    lower = dot_halves(second, halves(tall))
    bridge = dot_halves(second, across)
    lower_left = lower[:, : half + head_size] - dot_halves(halves(bridge), halves(upper))
    top = [upper[:, :half], jnp.zeros((half, half), F32), upper[:, half:]]
    bottom = [lower_left[:, :half], lower[:, half + head_size :], lower_left[:, half:]]
    return halves(
        jnp.concatenate([jnp.concatenate(top, axis=1), jnp.concatenate(bottom, axis=1)], axis=0)
    )


def lane_pieces(scores, size):
    return [score[:, i : i + size] for score in scores for i in range(0, score.shape[1], size)]


def row_peak(scores, peak):
    largest = functools.reduce(jnp.maximum, lane_pieces(scores, peak.shape[1]))
    return jnp.maximum(peak, jnp.max(largest, axis=1, keepdims=True))


def row_weights(scores, peak, rate):
    pieces = [jnp.exp2((piece - peak) * rate) for piece in lane_pieces(scores, peak.shape[1])]
    return jnp.concatenate(pieces, axis=1).astype(BF16)


def reciprocal(value):
    rough = pl.reciprocal(value, approx=True)
    return rough * (2.0 - value * rough)


def query_heads(heads, queries_ref, both_ref, ones_ref, solved, gain_ref, state_refs):
    turned_ref, peak_ref, total_ref, weighted_ref = state_refs
    length = ones_ref.shape[0]
    head_size = ones_ref.shape[1] // 2
    rate = math.log2(math.e) * head_size ** (-0.5)
    rows = lax.broadcasted_iota(jnp.int32, (length, length), 0)
    columns = lax.broadcasted_iota(jnp.int32, (length, length), 1)
    visible = rows >= columns
    gain = jnp.where(visible, gain_ref[0:1, :], 0.0)
    hidden = jnp.where(visible, 0.0, -1e30)
    both = both_ref[...]
    values = ones_ref[...]
    for head in heads:
        span = slice(head * head_size, (head + 1) * head_size)
        queries = queries_ref[:, span]
        faced = dot(queries, both)
        change = dot_halves(halves(faced[:, :length] * gain), solved)
        scores = (faced[:, length:] - change[:, :length]) + hidden
        turned_ref[:, span] = (queries.astype(F32) - change[:, length:]).astype(BF16)
        peak = jnp.broadcast_to(jnp.max(scores, axis=1, keepdims=True), (length, head_size))
        sums = dot(row_weights([scores], peak, rate), values)
        peak_ref[:, span] = peak
        weighted_ref[:, span] = sums[:, :head_size]
        total_ref[:, span] = sums[:, head_size:]


def first_queries(heads, *refs):
    queries_ref, both_ref, ones_ref, partial_ref, reflect_ref, gain_ref = refs[:6]
    *state_refs, solved_ref = refs[6:]
    solved = solve_rows(partial_ref, reflect_ref)
    wide_size = solved[0].shape[1]
    solved_ref[:, :wide_size] = solved[0]
    solved_ref[:, wide_size:] = solved[1]
    query_heads(heads, queries_ref, both_ref, ones_ref, solved, gain_ref, state_refs)


def other_queries(heads, longest, docs_hbm, *refs):
    queries_ref, both_ref, ones_ref, solved_ref, gain_ref = refs[:5]
    *state_refs, present_ref, docs_ref, docs_sem = refs[9:]
    docs_copy = pltpu.make_async_copy(docs_hbm, docs_ref, docs_sem)
    docs_copy.start()
    for done_ref, state_ref in zip(refs[5:9], state_refs):
        state_ref[:, : done_ref.shape[1]] = done_ref[...]
    wide_size = solved_ref.shape[1] // 2
    solved = (solved_ref[:, :wide_size], solved_ref[:, wide_size:])
    query_heads(heads, queries_ref, both_ref, ones_ref, solved, gain_ref, state_refs)
    docs_copy.wait()
    block = lax.axis_index("outer") * lax.axis_size("inner") + lax.axis_index("inner")
    own_doc = docs_ref[block]
    present = jnp.int32(0)
    for distance in range(1, longest):
        source = block - distance
        same = (source >= 0) & (docs_ref[jnp.maximum(source, 0)] == own_doc)
        present = present + same.astype(jnp.int32)
    state = 2 * present + block % 2
    present_ref[...] = jnp.full(present_ref.shape, state, jnp.int32)


def present_and_odd(present_ref):
    state = present_ref[0, 0]
    return state // 2, state % 2 == 1


def put_out(out_ref, out_hbm, out_sems, head, head_size):
    span = slice(head * head_size, (head + 1) * head_size)
    return pltpu.make_async_copy(out_ref.at[:, span], out_hbm.at[:, span], out_sems.at[head])


def attend(heads, state_refs, new_refs, all_keys, values, out_refs):
    turned_ref, peak_ref, total_ref, weighted_ref = state_refs
    head_size = values.shape[1] // 2
    rate = math.log2(math.e) * head_size ** (-0.5)
    for head in heads:
        span = slice(head * head_size, (head + 1) * head_size)
        old_peak = peak_ref[:, span]
        scores = [dot(turned_ref[:, span], keys) for keys in all_keys]
        peak = row_peak(scores, old_peak)
        sums = dot(row_weights(scores, peak, rate), values)
        factor = jnp.exp2((old_peak - peak) * rate)
        total = total_ref[:, span] * factor + sums[:, head_size:]
        weighted = weighted_ref[:, span] * factor + sums[:, :head_size]
        if out_refs is not None:
            out_refs[0][:, span] = (weighted * reciprocal(total)).astype(BF16)
            if len(out_refs) > 1:
                put_out(*out_refs, head, head_size).start()
        else:
            for new_ref, new in zip(new_refs, (peak, total, weighted)):
                new_ref[:, span] = new
    if out_refs is not None and len(out_refs) > 1:
        wait_out(heads, out_refs, head_size)


def finish(head_count, sum_refs, out_refs):
    total_ref, weighted_ref = sum_refs
    head_size = total_ref.shape[1] // head_count
    for head in range(head_count):
        span = slice(head * head_size, (head + 1) * head_size)
        out_refs[0][:, span] = (weighted_ref[:, span] * reciprocal(total_ref[:, span])).astype(BF16)
        put_out(*out_refs, head, head_size).start()
    wait_out(range(head_count), out_refs, head_size)


def wait_out(heads, out_refs, head_size):
    for head in heads:
        put_out(*out_refs, head, head_size).wait()


def store_values(values_ref, slot, place, packet, length):
    head_size = packet.shape[0]
    rows = pl.ds(place * length, length)
    start = length + head_size
    pieces = [
        packet[:, at : at + head_size] for at in range(start, start + length, head_size)
    ]
    values_ref[slot, rows, :head_size] = jnp.concatenate(pieces, axis=0)
    values_ref[slot, rows, head_size:] = jnp.ones((length, head_size), BF16)


def nearest(heads, old_refs, new_refs, packet_ref, values_ref, out_refs):
    packet = packet_ref[...]
    length = values_ref.shape[1]
    store_values(values_ref, 0, 0, packet, length)
    attend(heads, old_refs, new_refs, [packet[:, :length]], values_ref[0], out_refs)


def is_first_odd():
    return (lax.axis_index("outer") == 0) & (lax.axis_index("inner") == 1)


def early_kernel(heads, present_ref, beside_ref, *refs):
    *state_refs, done_ref, values_ref = refs
    present, _ = present_and_odd(present_ref)

    @pl.when(is_first_odd() & (present == 1))
    def _():
        nearest(heads, state_refs, None, beside_ref, values_ref, (done_ref,))


def nearest_kernel(head_count, early_heads, present_ref, beside_ref, done_ref, *refs):
    old_refs, new_refs = refs[:4], refs[4:7]
    out_hbm, out_ref, values_ref, out_sems = refs[7:]
    out_refs = (out_ref, out_hbm, out_sems)
    present, odd = present_and_odd(present_ref)
    first_odd = is_first_odd()
    heads = range(head_count)

    @pl.when(present == 0)
    def _():
        finish(head_count, old_refs[2:], out_refs)

    @pl.when(first_odd & (present == 1))
    def _():
        head_size = beside_ref.shape[0]
        done_refs = (done_ref, out_hbm, out_sems)
        for head in heads[:early_heads]:
            put_out(*done_refs, head, head_size).start()
        if early_heads < head_count:
            nearest(heads[early_heads:], old_refs, new_refs, beside_ref, values_ref, out_refs)
        wait_out(heads[:early_heads], done_refs, head_size)

    @pl.when(odd & (present == 1) & jnp.logical_not(first_odd))
    def _():
        nearest(heads, old_refs, new_refs, beside_ref, values_ref, out_refs)

    @pl.when(odd & (present > 1))
    def _():
        nearest(heads, old_refs, new_refs, beside_ref, values_ref, None)

    @pl.when(jnp.logical_not(odd) & (present > 0))
    def _():
        for old_ref, new_ref in zip(old_refs[1:], new_refs):
            new_ref[...] = old_ref[...]


def earlier_kernel(head_count, longest, present_ref, *refs):
    packet_refs = refs[:longest]
    state_refs = refs[longest : longest + 4]
    out_hbm, out_ref, keys_ref, values_ref, out_sems = refs[-5:]
    out_refs = (out_ref, out_hbm, out_sems)
    present, odd = present_and_odd(present_ref)
    length = out_ref.shape[0]
    head_size = out_ref.shape[1] // head_count
    wide_size = length + head_size
    steps = longest // 2 - 1
    apart_refs, swapped_refs = packet_refs[:steps], packet_refs[steps : 2 * steps]
    mixed_ref, beside_ref = packet_refs[2 * steps :]
    slots = values_ref.shape[0]

    def packet_of(distance, known_odd):
        if distance % 2 == 0:
            return apart_refs[distance // 2 - 1][...]
        odd_ref = beside_ref if distance == 1 else swapped_refs[(distance - 1) // 2 - 1]
        even_ref = mixed_ref if distance == longest - 1 else swapped_refs[(distance + 1) // 2 - 1]
        if known_odd is None:
            return jnp.where(odd, odd_ref[...], even_ref[...])
        return (odd_ref if known_odd else even_ref)[...]

    def collect(first, last, known_odd=None):
        transit = None
        all_keys = []
        for distance in range(1, last + 1):
            packet = packet_of(distance, known_odd)
            keys = packet[:, :length]
            own_transit = packet[:, length:wide_size]
            if distance == 1:
                transit = own_transit
            elif distance == 2:
                keys = dot(transit, keys).astype(BF16)
                if distance < last:
                    transit = dot(transit, own_transit)
            else:
                high, low = halves(transit)
                keys = (dot(high, keys) + dot(low, keys)).astype(BF16)
                if distance < last:
                    transit = dot(high, own_transit) + dot(low, own_transit)
            if distance >= first:
                all_keys.append(keys)
                index = distance - first
                store_values(values_ref, index // GROUP, index % GROUP, packet, length)
        return all_keys

    def take(first, last, known_odd):
        keys = collect(first, last, known_odd)
        values = values_ref[0, : len(keys) * length, :]
        attend(range(head_count), state_refs, None, keys, values, out_refs)

    def choose(first, last, known_odd):
        if first == last:
            take(2 if known_odd else 1, last, known_odd)
        else:
            middle = (first + last + 1) // 2
            lax.cond(
                present >= middle,
                lambda: choose(middle, last, known_odd),
                lambda: choose(first, middle - 1, known_odd),
            )

    if slots == 1:

        work = (present > odd.astype(jnp.int32)).astype(jnp.int32)

        @pl.loop(0, work)
        def _(_):
            lax.cond(
                odd,
                lambda: choose(2, longest - 1, True),
                lambda: choose(1, longest - 1, False),
            )

    else:

        @pl.when(present > 0)
        def _():
            for index, keys in enumerate(collect(1, longest - 1)):
                slot, place = index // GROUP, index % GROUP
                keys_ref[slot, :, place * length : (place + 1) * length] = keys

        def visit(slot, blocks):
            keys = [keys_ref[slot, :, i * length : (i + 1) * length] for i in range(blocks)]
            values = values_ref[slot, : blocks * length, :]
            attend(range(head_count), state_refs, state_refs[1:], keys, values, None)

        full = present // GROUP

        @pl.loop(0, full)
        def _(slot):
            visit(slot, GROUP)

        for blocks in range(1, GROUP):
            pl.when(present % GROUP == blocks)(functools.partial(visit, full, blocks))
        finish(head_count, state_refs[2:], out_refs)


def vmem(count):
    return [pl.BlockSpec(memory_space=pltpu.VMEM)] * count


def in_hbm(value):
    return pltpu.with_memory_space_constraint(value, pltpu.HBM)


def permuted(value, target):
    count = lax.axis_size("outer") * lax.axis_size("inner")
    return lax.ppermute(value, AXES, [(i, target(i) % count) for i in range(count)])


def local(queries, keys, values, reflect, reflect_logit, doc_of_block):
    longest = lax.axis_size("outer") * lax.axis_size("inner") // 8
    length, head_size = keys.shape
    head_count = queries.shape[1] // head_size
    wide_size = length + head_size
    params = pltpu.CompilerParams(vmem_limit_bytes=VMEM_LIMIT)
    shape = jax.ShapeDtypeStruct
    hbm = pl.BlockSpec(memory_space=pltpu.HBM)
    packet, partial, gain, both, ones, reflect_rows = pl.pallas_call(
        key_kernel,
        out_shape=(
            shape((head_size, wide_size + length), BF16),
            shape((length // 2, 3 * length), F32),
            shape((8, length), F32),
            shape((head_size, 2 * length), BF16),
            shape((length, 2 * head_size), BF16),
            shape((length, head_size), BF16),
        ),
        in_specs=[hbm] * 4,
        out_specs=tuple(vmem(6)),
        scratch_shapes=[
            pltpu.VMEM((length, head_size), BF16),
            pltpu.VMEM((1, length), F32),
            pltpu.SemaphoreType.DMA((4,)),
        ],
        compiler_params=params,
        cost_estimate=pl.CostEstimate(
            flops=40 * length**3, bytes_accessed=8 * length * length, transcendentals=length
        ),
        name="key_side",
    )(*(in_hbm(value) for value in (reflect, keys, values, reflect_logit.reshape(1, length))))
    apart = [permuted(packet, lambda i, s=s: i + 2 * s) for s in range(1, longest // 2)]
    wide = shape(queries.shape, F32)
    state_shapes = (shape(queries.shape, BF16), wide, wide, wide)
    first = max(1, head_count // 4)
    first_shapes = [shape((length, first * head_size), part.dtype) for part in state_shapes]

    def query_cost(heads):
        return pl.CostEstimate(
            flops=heads * 10 * length**3,
            bytes_accessed=16 * length * length * heads,
            transcendentals=heads * length * length,
        )

    *state, solved = pl.pallas_call(
        functools.partial(first_queries, range(first)),
        out_shape=(*first_shapes, shape((length, 2 * wide_size), BF16)),
        in_specs=vmem(6),
        out_specs=tuple(vmem(5)),
        compiler_params=params,
        cost_estimate=query_cost(first),
        name="first_queries",
    )(queries, both, ones, partial, reflect_rows, gain)
    mixed_packet, state[0] = lax.optimization_barrier((packet, state[0]))
    beside = permuted(mixed_packet, lambda i: i ^ 1)
    mixed = permuted(mixed_packet, lambda i: i + longest - 1 if i % 2 else i + 1)
    slots = (longest - 1 + GROUP - 1) // GROUP
    one_values = pltpu.VMEM((1, length, 2 * head_size), BF16)
    *state, present = pl.pallas_call(
        functools.partial(other_queries, range(first, head_count), longest),
        out_shape=(*state_shapes, shape((8, 128), jnp.int32)),
        in_specs=[hbm] + vmem(9),
        out_specs=tuple(vmem(5)),
        scratch_shapes=[
            pltpu.SMEM(doc_of_block.shape, jnp.int32),
            pltpu.SemaphoreType.DMA(()),
        ],
        compiler_params=params,
        cost_estimate=query_cost(head_count - first),
        name="other_queries",
    )(in_hbm(doc_of_block), queries, both, ones, solved, gain, *state)
    out_shape = shape(queries.shape, BF16)
    slots = (longest - 1 + GROUP - 1) // GROUP
    one_values = pltpu.VMEM((1, length, 2 * head_size), BF16)
    out_scratch = [pltpu.VMEM(queries.shape, BF16), pltpu.SemaphoreType.DMA((head_count,))]
    nearest_cost = pl.CostEstimate(
        flops=head_count * 2 * length**3,
        bytes_accessed=4 * length * length * head_count,
        transcendentals=head_count * length * length,
    )
    turned = state[0]
    *apart, present = lax.optimization_barrier((*apart, present))
    early_heads = max(1, 3 * head_count // 4)
    if slots == 1:
        done = pl.pallas_call(
            functools.partial(early_kernel, range(early_heads)),
            out_shape=shape((length, early_heads * head_size), BF16),
            in_specs=vmem(6),
            out_specs=vmem(1)[0],
            scratch_shapes=[one_values],
            compiler_params=params,
            cost_estimate=pl.CostEstimate(flops=0, bytes_accessed=0, transcendentals=0),
            name="early_heads",
        )(present, beside, *state)
        *apart, done = lax.optimization_barrier((*apart, done))
    swapped = [permuted(moved, lambda i: i ^ 1) for moved in apart]
    sums, started = state[1:], []
    if slots == 1:
        *sums, out = pl.pallas_call(
            functools.partial(nearest_kernel, head_count, early_heads),
            out_shape=(*state_shapes[1:], out_shape),
            in_specs=vmem(7),
            out_specs=(*vmem(3), hbm),
            scratch_shapes=[out_scratch[0], one_values, out_scratch[1]],
            compiler_params=params,
            cost_estimate=nearest_cost,
            name="nearest_block",
        )(present, beside, done, *state)
        started = [in_hbm(out)]
    return pl.pallas_call(
        functools.partial(earlier_kernel, head_count, longest),
        out_shape=out_shape,
        in_specs=vmem(longest + 5) + [hbm] * len(started),
        out_specs=hbm,
        input_output_aliases={longest + 5: 0} if started else {},
        scratch_shapes=[
            out_scratch[0],
            pltpu.VMEM((slots, head_size, GROUP * length), BF16),
            pltpu.VMEM((slots, GROUP * length, 2 * head_size), BF16),
            out_scratch[1],
        ],
        compiler_params=params,
        cost_estimate=pl.CostEstimate(
            flops=head_count * 6 * length**3,
            bytes_accessed=16 * length * length * head_count,
            transcendentals=3 * head_count * length * length,
        ),
        name="earlier_blocks",
    )(present, *apart, *swapped, mixed, beside, turned, *sums, *started)


def solution(mesh):
    placed = (
        P(AXES, None),
        P(AXES, None),
        P(AXES, None),
        P(AXES, None),
        P(AXES),
        P(),
    )
    return jax.shard_map(
        local, mesh=mesh, in_specs=placed, out_specs=P(AXES, None), check_vma=False
    )
```
